256 devices in a mesh: loop: 32 (over x, y, core), tp: 8 (over z).
Axes of the slice: x: 4, y: 4, z: 8, core: 2. Of those that a mesh axis runs over, the one named last changes fastest.
Arguments:
- queries: bfloat16 [8192, 8192], P('loop', 'tp'), may hold values from -8 to 8
- key_values: bfloat16 [8192, 2048], P('loop', 'tp'), may hold values from -8 to 8
- prompt_ids: int32 [8192], P('loop'), may hold values from 0 to 15, never falling along the last dimension, each value on 1 to 2048 neighbouring positions
- out_weight: bfloat16 [8192, 4096], P('tp'), may hold values from -5 to 5
Outputs:
- mixed: bfloat16 [8192, 4096], P('loop', 'tp')
The draws below stay inside these ranges and needn't reach their ends.
Inputs may be any that keep to these rules, and one draw needn't show every extreme that they name: `prompt_ids`: prompt numbers never fall along the tokens; each prompt holds 1 to 2048 tokens and one holds exactly 2048.
All inputs are finite; a program needn't handle non-finite values.
Results may differ from the reference program's by a relative error of at most 0.018.
Values may be sent and summed in bfloat16 or wider, within the bound.
No kernel may reach another device: no remote copies, remote signals or barrier semaphores. Data moves between devices by JAX's collectives and lax.ppermute only.
A program may use at most 64 MiB of HBM per device.

```python
import math
import jax
import jax.numpy as jnp
import numpy as np
from jax import lax

HD = 128
GROUP = 8
D_OUT = 4096
STRETCH = 256
KV_HEADS = 8
Q_HEADS = 64
TOKENS = 8192
SPAN = 8
MOST = 2048
PROMPTS = 16
N_LOOP = 32
N_TP = 8


def draw_queries(key, part):
    key = jax.random.fold_in(key, 11)
    drawn_values = jnp.clip(jax.random.normal(key, (TOKENS, KV_HEADS * GROUP * HD), jnp.float32), -8.0, 8.0)
    return drawn_values.astype(jnp.bfloat16)


def draw_key_values(key, part):
    key = jax.random.fold_in(key, 12)
    drawn_values = jnp.clip(jax.random.normal(key, (TOKENS, KV_HEADS, 2, HD), jnp.float32), -8.0, 8.0)
    return drawn_values.reshape(TOKENS, KV_HEADS * 2 * HD).astype(jnp.bfloat16)


def raised(drawn, own_key, source, target, parts, factor):
    owner, partner = [(jnp.arange(drawn.shape[axis_at]) // (drawn.shape[axis_at] // parts)).reshape([-1 if axis == axis_at else 1 for axis in range(drawn.ndim)]) for axis_at in (source, target)]
    chosen = jax.random.permutation(own_key, parts)[partner]
    strong = (owner == chosen) | (owner == (partner + parts // 2) % parts)
    return jnp.where(strong, factor * drawn, drawn)


def levels(key, shape, split, least, high):
    level = 1.0
    for axis_at, parts in split:
        heights = jax.random.uniform(jax.random.fold_in(jax.random.fold_in(key, 6), axis_at), (parts,), jnp.float32, least / len(split), high / len(split))
        level = level * jnp.repeat(jnp.exp(heights), shape[axis_at] // parts).reshape((-1,) + (1,) * (len(shape) - 1 - axis_at))
    return level


def length_profile(number_of, total, reach, skew):
    loads = [(1 << 20) // math.isqrt(rank ** skew) + 1 for rank in range(2, number_of + 1)]
    surplus, given = total - reach - (number_of - 1), [1] * (number_of - 1)
    while surplus > 0:
        candidates = [i for i in range(number_of - 1) if given[i] < reach]
        whole, left = sum([loads[i] for i in candidates]), surplus
        for i in candidates:
            extra = min(reach - given[i], max(1, left * loads[i] // whole), surplus)
            given[i] = given[i] + extra
            surplus = surplus - extra
    return np.array([reach] + given)


def ragged_sizes(own_key, number_of, total, most, slope):
    if number_of == 2:
        one = jax.random.randint(own_key, (), max(1, total - most), min(most, total - 1) + 1)
        return jnp.stack([one, total - one])
    lengths = jnp.asarray(length_profile(number_of, total, most, slope), jnp.int32)
    pairs = (number_of - 1) // 2
    source_of, taker = lengths[1:1 + 2 * pairs:2], lengths[2:2 + 2 * pairs:2]
    room = jnp.minimum(source_of - 1, most - taker)
    moved = jax.random.randint(jax.random.fold_in(own_key, 1), (pairs,), 0, 1 << 20) % (room + 1)
    lengths = lengths.at[1:1 + 2 * pairs:2].set(source_of - moved).at[2:2 + 2 * pairs:2].set(taker + moved)
    return lengths[jax.random.permutation(jax.random.fold_in(own_key, 2), number_of)]


def noise_with(stream_key, extent, deviation, most, shards, heavy, held_as=jnp.bfloat16):
    values = deviation * jax.random.normal(stream_key, extent, jnp.float32)
    if shards:
        values = values * levels(stream_key, extent, shards, -0.22, 0.18)
    return jnp.clip(raised(values, jax.random.fold_in(stream_key, 3), *heavy), -most, most).astype(held_as)


def setup_inputs(seed: int = 0) -> dict:
    arg_keys = jax.random.split(jax.random.key(seed), 5)
    return {
        "queries": draw_queries(jax.random.fold_in(arg_keys[4], 71), 0),
        "key_values": draw_key_values(jax.random.fold_in(arg_keys[4], 71), 0),
        "prompt_ids": jnp.searchsorted(jnp.cumsum(ragged_sizes(arg_keys[2], PROMPTS, TOKENS, MOST, 1)), jnp.arange(TOKENS), side="right").astype(jnp.int32),
        "out_weight": noise_with(arg_keys[3], (Q_HEADS * HD, D_OUT), 0.25, 5.0, ((0, 8),), (0, 1, 8, 2.0)),
    }


masked_score = -1e+30

def reference(queries, key_values, prompt_ids, out_weight):
    pad_rows = SPAN * STRETCH
    paired = key_values.reshape(TOKENS, KV_HEADS, 2, HD)
    padded_keys = jnp.pad(paired[:, :, 0, :], ((pad_rows, 0), (0, 0), (0, 0)))
    padded_values = jnp.pad(paired[:, :, 1, :], ((pad_rows, 0), (0, 0), (0, 0)))
    padded_ids = jnp.pad(prompt_ids, (pad_rows, 0), constant_values=-1).astype(jnp.int32)
    padded_pos = (jnp.arange(TOKENS + pad_rows, dtype=jnp.int32) - pad_rows).astype(jnp.int32)
    scaler = 1.0 / math.sqrt(HD)

    def one_stretch(stretch_index):
        start = (stretch_index * STRETCH).astype(jnp.int32)
        query_block = lax.dynamic_slice_in_dim(queries, start, STRETCH, 0).reshape(STRETCH, KV_HEADS, GROUP, HD).astype(jnp.float32)
        key_rows = lax.dynamic_slice_in_dim(padded_keys, start, pad_rows + STRETCH, 0).astype(jnp.float32)
        value_rows = lax.dynamic_slice_in_dim(padded_values, start, pad_rows + STRETCH, 0).astype(jnp.float32)
        key_ids = lax.dynamic_slice_in_dim(padded_ids, start, pad_rows + STRETCH, 0)
        key_pos = lax.dynamic_slice_in_dim(padded_pos, start, pad_rows + STRETCH, 0)
        query_ids = lax.dynamic_slice_in_dim(prompt_ids, start, STRETCH, 0)
        query_pos = start + jnp.arange(STRETCH, dtype=jnp.int32)
        scores = jnp.einsum('qhgd,khd->hgqk', query_block, key_rows) * scaler
        allowed = (query_ids[:, None] == key_ids[None, :]) & (key_pos[None, :] <= query_pos[:, None])
        scores = jnp.where(allowed, scores, masked_score)
        row_max = lax.optimization_barrier(jnp.max(scores, axis=-1, keepdims=True))
        probs = jnp.where(allowed, jnp.exp(scores - row_max), 0.0)
        summed = lax.optimization_barrier(jnp.sum(probs, axis=-1))
        probs_low = probs.astype(jnp.bfloat16).astype(jnp.float32)
        weighted = jnp.einsum('hgqk,khd->hgqd', probs_low, value_rows) / summed[..., None]
        return jnp.transpose(weighted, (2, 0, 1, 3)).reshape(STRETCH, Q_HEADS * HD).astype(jnp.bfloat16)
    attention = lax.map(one_stretch, jnp.arange(N_LOOP, dtype=jnp.int32)).reshape(TOKENS, Q_HEADS * HD)
    attention_split = attention.reshape(TOKENS, N_TP, Q_HEADS * HD // N_TP)
    weight_split = out_weight.reshape(N_TP, Q_HEADS * HD // N_TP, D_OUT)

    def add_part(running, tp_index):
        product = jnp.dot(attention_split[:, tp_index, :], weight_split[tp_index], preferred_element_type=jnp.float32)
        product = lax.optimization_barrier(product.astype(jnp.bfloat16)).astype(jnp.float32)
        return (running + product, None)
    running, unused = lax.scan(add_part, jnp.zeros((TOKENS, D_OUT), jnp.float32), jnp.arange(N_TP, dtype=jnp.int32))
    return running.astype(jnp.bfloat16)
```

```python
import functools
import math

import jax
import jax.numpy as jnp
from jax import lax
from jax.experimental import pallas as pl
from jax.experimental.pallas import tpu as pltpu
from jax.sharding import PartitionSpec as P

HD = 128
HEADS = 8
TOK = 256
PART = 128
ROWS = HEADS * PART
PIECE = TOK + 16
CHUNK = 512
SCALE = 1.0 / math.sqrt(HD)
MASKED = -1e30
F32 = jnp.float32
BF16 = jnp.bfloat16


def attend(valid, queries, ids, pieces, before, after, scores, peak, query_rows, own_first):
    count = len(pieces)
    for head in range(HEADS):
        query_rows[pl.ds(head * PART, PART), :] = queries[:, pl.ds(head * HD, HD)]
    own_ids = ids[...]
    masks = []
    for at, (which, piece) in enumerate(pieces):
        key_ids = piece[TOK:PIECE, :][0:1, :].astype(F32)
        key_ids = jnp.where(valid[which] > 0, key_ids, -1.0)
        allowed = own_ids == key_ids
        if own_first is not None and at == 0:
            rows = lax.broadcasted_iota(jnp.int32, (PART, TOK), 0) + own_first
            allowed = allowed & (lax.broadcasted_iota(jnp.int32, (PART, TOK), 1) <= rows)
        masks.append(allowed)
    for head in range(HEADS):
        rows = pl.ds(head * PART, PART)
        best = None
        for at, (_, piece) in enumerate(pieces):
            found = lax.dot_general(
                query_rows[rows, :],
                piece[0:TOK, 0:HD],
                (((1,), (1,)), ((), ())),
                preferred_element_type=F32,
            )
            found = jnp.where(masks[at], found, MASKED)
            scores[rows, at * TOK : (at + 1) * TOK] = found
            here = jnp.maximum(found[:, :HD], found[:, HD:])
            best = here if best is None else jnp.maximum(best, here)
        peak[rows, :] = best
    ones = jnp.ones((TOK, HD), BF16)
    values = jnp.concatenate(
        [jnp.concatenate([piece[0:TOK, HD:], ones], axis=1) for _, piece in pieces], axis=0
    )
    for head in range(HEADS):
        rows = pl.ds(head * PART, PART)
        top = jnp.broadcast_to(jnp.max(peak[rows, :], axis=1, keepdims=True), (PART, HD))
        if before is not None:
            old = before[0][rows, :]
            top = jnp.maximum(top, old)
        wide = jnp.concatenate([top] * (2 * count), axis=1)
        probs = jnp.exp((scores[rows, 0 : count * TOK] - wide) * SCALE).astype(BF16)
        added = jnp.dot(probs, values, preferred_element_type=F32)
        if before is not None:
            shrink = jnp.exp((old - top) * SCALE)
            added = added + before[1][rows, :] * jnp.concatenate([shrink, shrink], axis=1)
        after(head, rows, top, added)


def early_kernel(parts, which, first, *refs):
    valid, queries, ids = refs[:3]
    pieces = list(zip(which, refs[3 : 3 + len(which)]))
    at = 3 + len(which)
    if not first:
        before = refs[at : at + 2 * parts]
        at += 2 * parts
    after = refs[at : at + 2 * parts]
    scores, peak, query_rows = refs[at + 2 * parts :]
    for part in range(parts):
        tops, sums = after[2 * part : 2 * part + 2]

        def keep(head, rows, top, added):
            tops[rows, :] = top
            sums[rows, :] = added

        attend(
            valid,
            queries.at[pl.ds(part * PART, PART)],
            ids.at[pl.ds(part * PART, PART)],
            pieces,
            None if first else before[2 * part : 2 * part + 2],
            keep,
            scores,
            peak,
            query_rows,
            part * PART if first else None,
        )


def last_kernel(part, which, *refs):
    valid, columns, queries, ids = refs[:4]
    pieces = list(zip(which, refs[4 : 4 + len(which)]))
    tops, sums, weight, attention, product, scores, peak, query_rows = refs[4 + len(which) :]

    def finish(head, rows, top, added):
        share = added[:, :HD] / added[:, HD:]
        attention[:, pl.ds(head * HD, HD)] = share.astype(BF16)

    attend(
        valid,
        queries.at[pl.ds(part * PART, PART)],
        ids.at[pl.ds(part * PART, PART)],
        pieces,
        (tops, sums),
        finish,
        scores,
        peak,
        query_rows,
        None,
    )
    start = pl.multiple_of(columns[0] * CHUNK, CHUNK)
    product[...] = jnp.dot(
        attention[...], weight[:, pl.ds(start, CHUNK)], preferred_element_type=F32
    ).astype(BF16)


def project_kernel(columns, own, mate, weight, *outs):
    both = jnp.concatenate([own[...], mate[...]], axis=0)
    for at, out in enumerate(outs):
        rows = both if out.shape[0] == 2 * PART else own[...]
        start = pl.multiple_of(columns[at + 1] * CHUNK, CHUNK)
        out[...] = jnp.dot(
            rows, weight[:, pl.ds(start, CHUNK)], preferred_element_type=F32
        ).astype(BF16)


VMEM = pl.BlockSpec(memory_space=pltpu.VMEM)
SMEM = pl.BlockSpec(memory_space=pltpu.SMEM)
PARAMS = pltpu.CompilerParams(vmem_limit_bytes=48 << 20)


def scratch(count):
    return [
        pltpu.VMEM((ROWS, count * TOK), F32),
        pltpu.VMEM((ROWS, HD), F32),
        pltpu.VMEM((ROWS, HD), BF16),
    ]


def costs(flops, size):
    return pl.CostEstimate(flops=int(flops), bytes_accessed=int(size), transcendentals=0)


def early(valid, queries, ids, pieces, state):
    which = [item[0] for item in pieces]
    parts = TOK // PART
    shapes = [jax.ShapeDtypeStruct((ROWS, HD), F32), jax.ShapeDtypeStruct((ROWS, 2 * HD), F32)]
    given = [] if state is None else list(state)
    fixed = 3 + len(which)
    return pl.pallas_call(
        functools.partial(early_kernel, parts, which, state is None),
        out_shape=shapes * parts,
        in_specs=[SMEM] + [VMEM] * (2 + len(which) + len(given)),
        out_specs=[VMEM] * (2 * parts),
        scratch_shapes=scratch(len(which)),
        input_output_aliases={fixed + i: i for i in range(len(given))},
        compiler_params=PARAMS,
        cost_estimate=costs(1.2e9 * len(which), 1 << 20),
        name="attend_early",
    )(valid, queries, ids, *[item[1] for item in pieces], *given)


def last(part, valid, columns, queries, ids, pieces, state, weight):
    which = [item[0] for item in pieces]
    return pl.pallas_call(
        functools.partial(last_kernel, part, which),
        out_shape=[
            jax.ShapeDtypeStruct((PART, HEADS * HD), BF16),
            jax.ShapeDtypeStruct((PART, CHUNK), BF16),
        ],
        in_specs=[SMEM, SMEM] + [VMEM] * (5 + len(which)),
        out_specs=[VMEM] * 2,
        scratch_shapes=scratch(len(which)),
        compiler_params=PARAMS,
        cost_estimate=costs(0.6e9 * len(which), 1 << 20),
        name="attend_last",
    )(valid, columns, queries, ids, *[item[1] for item in pieces], *state, weight)


def project(columns, own, mate, weight):
    wide = jax.ShapeDtypeStruct((2 * PART, CHUNK), BF16)
    return pl.pallas_call(
        project_kernel,
        out_shape=[wide, wide, wide, jax.ShapeDtypeStruct((PART, CHUNK), BF16)],
        in_specs=[SMEM] + [VMEM] * 3,
        out_specs=[VMEM] * 4,
        compiler_params=PARAMS,
        cost_estimate=costs(1.0e9, 1 << 20),
        name="project",
    )(columns, own, mate, weight)


def per_device(queries, key_values, prompt_ids, out_weight):
    stretches, ring = lax.axis_size("loop"), lax.axis_size("tp")
    place, tp = lax.axis_index("loop"), lax.axis_index("tp")
    core, chip = place % 2, place // 2

    def to_mate(value):
        return lax.ppermute(value, "loop", [(i, i ^ 1) for i in range(stretches)])

    def from_chip(value, steps):
        pairs = [(i, (i + 2 * steps) % stretches) for i in range(stretches)]
        return lax.ppermute(value, "loop", pairs)

    def along(value):
        pairs = []
        for loop in range(stretches):
            step = 1 if loop % 2 else ring - 1
            for z in range(ring):
                pairs.append((loop * ring + z, loop * ring + (z + step) % ring))
        return lax.ppermute(value, ("loop", "tp"), pairs)

    ids_row = jnp.pad(prompt_ids.astype(BF16)[None, :], ((0, PIECE - TOK - 1), (0, 0)))
    own = jnp.concatenate([key_values, ids_row], axis=0)
    ids = prompt_ids.astype(F32)[:, None]
    far = [4, 1, 2, 3]
    valid = jnp.stack([jnp.int32(1), core] + [(chip >= s).astype(jnp.int32) for s in (1, 2, 3, 4)])
    side = jnp.where(core == 0, 1, -1)
    columns = jnp.stack([tp + 4, tp + 4 + side, tp + 4 + 2 * side, tp + 4 + 3 * side, tp]) % ring

    received = {s: from_chip(own, s) for s in far}
    pairs = {0: [(0, own), (1, to_mate(own))]}
    for s in far:
        pairs[s] = [(1 + s, received[s]), (1 + s, to_mate(received[s]))]

    state = early(valid, queries, ids, pairs[0], None)
    state = early(valid, queries, ids, pairs[far[0]], state)
    state = early(valid, queries, ids, pairs[far[1]] + pairs[far[2]], state)

    outs = []
    for part in range(TOK // PART):
        attention, product = last(
            part, valid, columns, queries, ids, pairs[far[3]], state[2 * part : 2 * part + 2], out_weight
        )
        extra = along(product)
        one, two, three, mine = project(columns, attention, to_mate(attention), out_weight)
        moved = along(jnp.concatenate([one[:PART] + extra, one[PART:]], axis=0))
        moved = along(two + moved)
        moved = along(three + moved)
        other = to_mate(moved[PART:])
        total = mine.astype(F32) + moved[:PART].astype(F32) + other.astype(F32)
        outs.append(total.astype(BF16))
    return jnp.concatenate(outs, axis=0)


def solution(mesh):
    in_specs = (P("loop", "tp"), P("loop", "tp"), P("loop"), P("tp", None))
    out_specs = P("loop", "tp")
    return jax.shard_map(
        per_device, mesh=mesh, in_specs=in_specs, out_specs=out_specs, check_vma=False
    )
```

```python
import functools
import math

import jax
import jax.numpy as jnp
from jax import lax
from jax.experimental import pallas as pl
from jax.experimental.pallas import tpu as pltpu
from jax.sharding import PartitionSpec as P

HD = 128
HEADS = 8
TOK = 256
PART = 128
ROWS = HEADS * TOK
PIECE = TOK + 16
CHUNK = 512
SCALE = 1.0 / math.sqrt(HD)
MASKED = -1e30
F32 = jnp.float32
BF16 = jnp.bfloat16


def allowed_keys(valid, own_ids, which, piece, causal):
    key_ids = piece[TOK:PIECE, :][0:1, :].astype(F32)
    key_ids = jnp.where(valid[which] > 0, key_ids, -1.0)
    allowed = own_ids == key_ids
    if causal:
        shape = (own_ids.shape[0], TOK)
        rows = lax.broadcasted_iota(jnp.int32, shape, 0)
        allowed = allowed & (lax.broadcasted_iota(jnp.int32, shape, 1) <= rows)
    return allowed


def attend(valid, query_rows, ids, first, size, pieces, before, keep, scores, peak, causal=False):
    count = len(pieces)
    own_ids = ids[pl.ds(first, size), :]
    masks = [allowed_keys(valid, own_ids, which, piece, causal) for which, piece in pieces]
    for head in range(HEADS):
        rows = pl.ds(head * TOK + first, size)
        best = None
        for at, (_, piece) in enumerate(pieces):
            found = lax.dot_general(
                query_rows[rows, :],
                piece[0:TOK, 0:HD],
                (((1,), (1,)), ((), ())),
                preferred_element_type=F32,
            )
            found = jnp.where(masks[at], found, MASKED)
            scores[rows, at * TOK : (at + 1) * TOK] = found
            here = jnp.maximum(found[:, :HD], found[:, HD:])
            best = here if best is None else jnp.maximum(best, here)
        peak[rows, :] = best
    ones = jnp.ones((TOK, HD), BF16)
    values = jnp.concatenate(
        [jnp.concatenate([piece[0:TOK, HD:], ones], axis=1) for _, piece in pieces], axis=0
    )
    for head in range(HEADS):
        rows = pl.ds(head * TOK + first, size)
        top = jnp.broadcast_to(jnp.max(peak[rows, :], axis=1, keepdims=True), (size, HD))
        if before is not None:
            old = before[0][rows, :]
            top = jnp.maximum(top, old)
        wide = jnp.concatenate([top] * (2 * count), axis=1)
        probs = jnp.exp((scores[rows, 0 : count * TOK] - wide) * SCALE).astype(BF16)
        added = jnp.dot(probs, values, preferred_element_type=F32)
        if before is not None:
            shrink = jnp.exp((old - top) * SCALE)
            added = added + before[1][rows, :] * jnp.concatenate([shrink, shrink], axis=1)
        keep(head, rows, top, added)


def open_kernel(valid, queries, ids, piece, tops, sums, query_rows, scores, peak):
    for head in range(HEADS):
        query_rows[pl.ds(head * TOK, TOK), :] = queries[:, pl.ds(head * HD, HD)]

    def keep(head, rows, top, added):
        tops[rows, :] = top
        sums[rows, :] = added

    attend(valid, query_rows, ids, 0, TOK, [(0, piece)], None, keep, scores, peak, causal=True)


def middle_kernel(which, valid, query_rows, ids, *refs):
    pieces = list(zip(which, refs[: len(which)]))
    old_tops, old_sums, tops, sums, scores, peak = refs[len(which) :]

    def keep(head, rows, top, added):
        tops[rows, :] = top
        sums[rows, :] = added

    attend(valid, query_rows, ids, 0, TOK, pieces, (old_tops, old_sums), keep, scores, peak)


def last_kernel(part, which, valid, columns, query_rows, ids, *refs):
    pieces = list(zip(which, refs[: len(which)]))
    tops, sums, weight, attention, product, scores, peak = refs[len(which) :]

    def finish(head, rows, top, added):
        share = added[:, :HD] / added[:, HD:]
        attention[:, pl.ds(head * HD, HD)] = share.astype(BF16)

    attend(
        valid, query_rows, ids, part * PART, PART, pieces, (tops, sums), finish, scores, peak
    )
    group = pl.ds(pl.multiple_of(columns[0] * CHUNK, CHUNK), CHUNK)
    product[...] = jnp.dot(
        attention[...], weight[:, group], preferred_element_type=F32
    ).astype(BF16)


def project_kernel(columns, own, mate, weight, *outs):
    both = jnp.concatenate([own[...], mate[...]], axis=0)
    for at, out in enumerate(outs):
        rows = both if out.shape[0] == 2 * PART else own[...]
        group = pl.ds(pl.multiple_of(columns[at + 1] * CHUNK, CHUNK), CHUNK)
        out[...] = jnp.dot(rows, weight[:, group], preferred_element_type=F32).astype(BF16)


VMEM = pl.BlockSpec(memory_space=pltpu.VMEM)
SMEM = pl.BlockSpec(memory_space=pltpu.SMEM)
PARAMS = pltpu.CompilerParams(vmem_limit_bytes=24 << 20)
STATE = [jax.ShapeDtypeStruct((ROWS, HD), F32), jax.ShapeDtypeStruct((ROWS, 2 * HD), F32)]


def scratch(count):
    return [pltpu.VMEM((ROWS, count * TOK), F32), pltpu.VMEM((ROWS, HD), F32)]


def costs(flops, size):
    return pl.CostEstimate(flops=int(flops), bytes_accessed=int(size), transcendentals=0)


def opening(valid, queries, ids, piece):
    outs = pl.pallas_call(
        open_kernel,
        out_shape=STATE + [jax.ShapeDtypeStruct((ROWS, HD), BF16)],
        in_specs=[SMEM] + [VMEM] * 3,
        out_specs=[VMEM] * 3,
        scratch_shapes=scratch(1),
        compiler_params=PARAMS,
        cost_estimate=costs(1e6, 1 << 10),
        name="attend_own",
    )(valid, queries, ids, piece)
    return outs[:2], outs[2]


def middle(valid, query_rows, ids, pieces, state):
    which = [item[0] for item in pieces]
    fixed = 3 + len(which)
    return pl.pallas_call(
        functools.partial(middle_kernel, which),
        out_shape=STATE,
        in_specs=[SMEM] + [VMEM] * (4 + len(which)),
        out_specs=[VMEM] * 2,
        scratch_shapes=scratch(len(which)),
        input_output_aliases={fixed: 0, fixed + 1: 1},
        compiler_params=PARAMS,
        cost_estimate=costs(1e6, 1 << 10),
        name="attend_more",
    )(valid, query_rows, ids, *[item[1] for item in pieces], *state)


def last(part, valid, columns, query_rows, ids, pieces, state, weight):
    which = [item[0] for item in pieces]
    return pl.pallas_call(
        functools.partial(last_kernel, part, which),
        out_shape=[
            jax.ShapeDtypeStruct((PART, HEADS * HD), BF16),
            jax.ShapeDtypeStruct((PART, CHUNK), BF16),
        ],
        in_specs=[SMEM, SMEM] + [VMEM] * (5 + len(which)),
        out_specs=[VMEM] * 2,
        scratch_shapes=scratch(len(which)),
        compiler_params=PARAMS,
        cost_estimate=costs(1.5e9, 1 << 20),
        name="attend_last",
    )(valid, columns, query_rows, ids, *[item[1] for item in pieces], *state, weight)


def project(columns, own, mate, weight):
    wide = jax.ShapeDtypeStruct((2 * PART, CHUNK), BF16)
    return pl.pallas_call(
        project_kernel,
        out_shape=[wide, wide, wide, jax.ShapeDtypeStruct((PART, CHUNK), BF16)],
        in_specs=[SMEM] + [VMEM] * 3,
        out_specs=[VMEM] * 4,
        compiler_params=PARAMS,
        cost_estimate=costs(1.5e9, 1 << 20),
        name="project",
    )(columns, own, mate, weight)


def per_device(queries, key_values, prompt_ids, out_weight):
    stretches, ring = lax.axis_size("loop"), lax.axis_size("tp")
    place, tp = lax.axis_index("loop"), lax.axis_index("tp")
    core, chip = place % 2, place // 2
    row = 8

    def to_mate(value):
        return lax.ppermute(value, "loop", [(i, i ^ 1) for i in range(stretches)])

    def from_chip(value, steps):
        pairs = [(i, (i + 2 * steps) % stretches) for i in range(stretches)]
        return lax.ppermute(value, "loop", pairs)

    def along_row(value, steps):
        pairs = [(i, i // row * row + (i + 2 * steps) % row) for i in range(stretches)]
        return lax.ppermute(value, "loop", pairs)

    def along(value):
        pairs = []
        for loop in range(stretches):
            step = 1 if loop % 2 else ring - 1
            for z in range(ring):
                pairs.append((loop * ring + z, loop * ring + (z + step) % ring))
        return lax.ppermute(value, ("loop", "tp"), pairs)

    ids_row = jnp.broadcast_to(prompt_ids.astype(BF16)[None, :], (PIECE - TOK, TOK))
    own = jnp.concatenate([key_values, ids_row], axis=0)
    ids = prompt_ids.astype(F32)[:, None]
    there = [(chip >= s).astype(jnp.int32) for s in (1, 2, 3, 4)]
    valid = jnp.stack([jnp.int32(1)] + there + [jnp.maximum(core, there[3])])
    side = jnp.where(core == 0, 1, -1)
    columns = jnp.stack([tp + 4, tp + 4 + side, tp + 4 + 2 * side, tp + 4 + 3 * side, tp]) % ring

    chip4 = from_chip(own, 4)
    chip1 = from_chip(own, 1)
    chip2 = from_chip(own, 2)
    state, query_rows = opening(valid, queries, ids, own)
    (chip4, state) = lax.optimization_barrier((chip4, state))
    chip3 = along_row(jnp.where(chip % 4 == 0, own, chip4), 3)
    beside = to_mate(jnp.where(core == 0, own, chip4))
    mate1 = to_mate(chip1)
    state = middle(valid, query_rows, ids, [(4, chip4), (5, beside)], state)
    (chip2, chip3, state) = lax.optimization_barrier((chip2, chip3, state))
    mate2 = to_mate(chip2)
    mate3 = to_mate(chip3)
    near = [(1, chip1), (1, mate1), (2, chip2), (2, mate2)]
    state = middle(valid, query_rows, ids, near, state)

    outs = []
    for part in range(TOK // PART):
        attention, product = last(
            part, valid, columns, query_rows, ids, [(3, chip3), (3, mate3)], state, out_weight
        )
        extra = along(product)
        one, two, three, mine = project(columns, attention, to_mate(attention), out_weight)
        moved = along(jnp.concatenate([one[:PART] + extra, one[PART:]], axis=0))
        moved = along(two + moved)
        moved = along(three + moved)
        other = to_mate(moved[PART:])
        total = mine.astype(F32) + moved[:PART].astype(F32) + other.astype(F32)
        outs.append(total.astype(BF16))
    return jnp.concatenate(outs, axis=0)


def solution(mesh):
    in_specs = (P("loop", "tp"), P("loop", "tp"), P("loop"), P("tp", None))
    out_specs = P("loop", "tp")
    return jax.shard_map(
        per_device, mesh=mesh, in_specs=in_specs, out_specs=out_specs, check_vma=False
    )
```

```python
import functools
import math

import jax
import jax.numpy as jnp
from jax import lax
from jax.experimental import pallas as pl
from jax.experimental.pallas import tpu as pltpu
from jax.sharding import PartitionSpec as P

HD = 128
HEADS = 8
TOK = 256
PART = 128
ROWS = HEADS * TOK
STEP = 256
PIECE = TOK + 16
CHUNK = 512
ROW = 8
SCALE = 1.0 / math.sqrt(HD)
MASKED = -1e30
F32 = jnp.float32
BF16 = jnp.bfloat16
BESIDE = -1


def place():
    at = lax.axis_index("loop")
    return at // 2, at % 2


def usable(back):
    chip, core = place()
    if back == 0:
        return jnp.bool_(True)
    if back == BESIDE:
        return (chip >= 4) | (core == 1)
    return chip >= back


def pack_kernel(key_values, ids, message):
    message[0:TOK, :] = key_values[...]
    row = jnp.broadcast_to(ids[...].astype(F32), (PIECE - TOK, TOK))
    message[TOK:PIECE, :] = row.astype(BF16)


def column_kernel(message, again, column):
    again[...] = message[...]
    square = (TOK, TOK)
    diagonal = lax.broadcasted_iota(jnp.int32, square, 0) == lax.broadcasted_iota(
        jnp.int32, square, 1
    )
    wide = jnp.broadcast_to(message[TOK:PIECE, :][0:1, :].astype(F32), square)
    column[...] = jnp.sum(jnp.where(diagonal, wide, 0.0), axis=1, keepdims=True)


def pick_kernel(own, far, ids, relayed, beside, ids_again):
    chip, core = place()
    ids_again[...] = ids[...]

    @pl.when(chip % 4 == 0)
    def _():
        relayed[...] = own[...]

    @pl.when(chip % 4 != 0)
    def _():
        relayed[...] = far[...]

    @pl.when(core == 0)
    def _():
        beside[...] = own[...]

    @pl.when(core != 0)
    def _():
        beside[...] = far[...]


def find_scores(query_rows, ids, part, pieces, scores, peak, base):
    own_ids = ids[pl.ds(part * PART, PART), :]
    own_ids = jnp.concatenate([own_ids] * (STEP // PART), axis=0)
    names = []
    for back, piece in pieces:
        key_ids = piece[TOK:PIECE, :][0:1, :].astype(F32)
        names.append(jnp.where(usable(back), key_ids, -1.0))
    for step in range(HEADS * PART // STEP):
        rows = pl.ds(part * HEADS * PART + step * STEP, STEP)
        out = pl.ds(base + step * STEP, STEP)
        best = None
        for at, (back, piece) in enumerate(pieces):
            found = lax.dot_general(
                query_rows[rows, :],
                piece[0:TOK, 0:HD],
                (((1,), (1,)), ((), ())),
                preferred_element_type=F32,
            )
            allowed = own_ids == names[at]
            if back == 0:
                shape = (STEP, TOK)
                token = lax.broadcasted_iota(jnp.int32, shape, 0) % PART + part * PART
                allowed = allowed & (lax.broadcasted_iota(jnp.int32, shape, 1) <= token)
            found = jnp.where(allowed, found, MASKED)
            scores[out, at * TOK : (at + 1) * TOK] = found
            here = jnp.maximum(found[:, :HD], found[:, HD:])
            best = here if best is None else jnp.maximum(best, here)
        peak[out, :] = best


def keep_values(pieces, values):
    for at, (_, piece) in enumerate(pieces):
        values[at * TOK : (at + 1) * TOK, 0:HD] = piece[0:TOK, HD:]
    values[:, HD:] = jnp.ones((values.shape[0], HD), BF16)


def own_kernel(queries, ids, piece, query_rows, scores, peak, values):
    for part in range(TOK // PART):
        for head in range(HEADS):
            rows = pl.ds((part * HEADS + head) * PART, PART)
            query_rows[rows, :] = queries[pl.ds(part * PART, PART), pl.ds(head * HD, HD)]
    keep_values([(0, piece)], values)
    for part in range(TOK // PART):
        find_scores(query_rows, ids, part, [(0, piece)], scores, peak, part * HEADS * PART)


def more_kernel(backs, query_rows, ids, *refs):
    pieces = list(zip(backs, refs[: len(backs)]))
    scores, peak, values = refs[len(backs) :]
    keep_values(pieces, values)
    for part in range(TOK // PART):
        find_scores(query_rows, ids, part, pieces, scores, peak, part * HEADS * PART)


def last_kernel(part, backs, early, query_rows, ids, *refs):
    pieces = list(zip(backs, refs[: len(backs)]))
    refs = refs[len(backs) :]
    kept = [refs[3 * at : 3 * at + 3] for at in range(early)]
    weight, attention, product, scores, peak, values = refs[3 * early :]
    keep_values(pieces, values)
    find_scores(query_rows, ids, part, pieces, scores, peak, 0)
    for step in range(HEADS * PART // STEP):
        rows = pl.ds(step * STEP, STEP)
        given = pl.ds(part * HEADS * PART + step * STEP, STEP)
        top = peak[rows, :]
        for _, other, _ in kept:
            top = jnp.maximum(top, other[given, :])
        top = jnp.broadcast_to(jnp.max(top, axis=1, keepdims=True), (STEP, HD))
        total = None
        for block, keys in [(s[given, :], v) for s, _, v in kept] + [(scores[rows, :], values)]:
            wide = jnp.concatenate([top] * (block.shape[1] // HD), axis=1)
            probs = jnp.exp((block - wide) * SCALE).astype(BF16)
            added = jnp.dot(probs, keys[...], preferred_element_type=F32)
            total = added if total is None else total + added
        share = (total[:, :HD] / total[:, HD:]).astype(BF16)
        for at in range(STEP // PART):
            head = step * (STEP // PART) + at
            attention[:, pl.ds(head * HD, HD)] = share[at * PART : (at + 1) * PART, :]
    group = lax.rem(lax.axis_index("tp") + 4, 8)
    group = pl.ds(pl.multiple_of(group * CHUNK, CHUNK), CHUNK)
    product[...] = jnp.dot(
        attention[...], weight[:, group], preferred_element_type=F32
    ).astype(BF16)


def project_kernel(own, mate, weight, *outs):
    both = jnp.concatenate([own[...], mate[...]], axis=0)
    side = 1 - 2 * place()[1]
    for at, out in enumerate(outs):
        if out.shape[0] == 2 * PART:
            rows, group = both, lax.axis_index("tp") + 4 + (at + 1) * side
        else:
            rows, group = own[...], lax.axis_index("tp")
        group = lax.rem(group, 8)
        group = pl.ds(pl.multiple_of(group * CHUNK, CHUNK), CHUNK)
        out[...] = jnp.dot(rows, weight[:, group], preferred_element_type=F32).astype(BF16)


def finish_kernel(*refs):
    out = refs[-1]
    for part in range(TOK // PART):
        mine, moved, other = refs[3 * part : 3 * part + 3]
        total = mine[...].astype(F32) + moved[0:PART, :].astype(F32) + other[...].astype(F32)
        out[pl.ds(part * PART, PART), :] = total.astype(BF16)


VMEM = pl.BlockSpec(memory_space=pltpu.VMEM)
PARAMS = pltpu.CompilerParams(vmem_limit_bytes=12 << 20)


def shape(rows, columns, kind=BF16):
    return jax.ShapeDtypeStruct((rows, columns), kind)


def call(kernel, name, micros, outs, *args, scratch=()):
    return pl.pallas_call(
        kernel,
        out_shape=outs,
        in_specs=[VMEM] * len(args),
        out_specs=[VMEM] * len(outs) if isinstance(outs, list) else VMEM,
        scratch_shapes=list(scratch),
        compiler_params=PARAMS,
        cost_estimate=pl.CostEstimate(
            flops=int(micros * 1e9), bytes_accessed=1 << 10, transcendentals=0
        ),
        name=name,
    )(*args)


def kept_shapes(count):
    return [shape(ROWS, count * TOK, F32), shape(ROWS, HD, F32), shape(count * TOK, 2 * HD)]


def per_device(queries, key_values, prompt_ids, out_weight):
    stretches, ring = lax.axis_size("loop"), lax.axis_size("tp")

    def to_mate(value):
        return lax.ppermute(value, "loop", [(i, i ^ 1) for i in range(stretches)])

    def from_chip(value, steps):
        pairs = [(i, (i + 2 * steps) % stretches) for i in range(stretches)]
        return lax.ppermute(value, "loop", pairs)

    def along_row(value, steps):
        pairs = [(i, i // ROW * ROW + (i + 2 * steps) % ROW) for i in range(stretches)]
        return lax.ppermute(value, "loop", pairs)

    def along(value):
        pairs = []
        for loop in range(stretches):
            step = 1 if loop % 2 else ring - 1
            for z in range(ring):
                pairs.append((loop * ring + z, loop * ring + (z + step) % ring))
        return lax.ppermute(value, ("loop", "tp"), pairs)

    piece = shape(PIECE, TOK)
    column = shape(TOK, 1, F32)
    own = call(pack_kernel, "pack", 0.5, piece, key_values, prompt_ids[None, :])
    chip4 = from_chip(own, 4)
    again, ids = call(column_kernel, "column", 0.3, [piece, column], own)
    chip1, chip2 = from_chip(again, 1), from_chip(again, 2)
    query_rows, *kept = call(
        own_kernel, "own_scores", 1.5, [shape(ROWS, HD)] + kept_shapes(1), queries, ids, again
    )
    (chip4, kept) = lax.optimization_barrier((chip4, kept))
    relayed, beside, ids = call(
        pick_kernel, "pick", 0.3, [piece, piece, column], again, chip4, ids
    )
    (chip1, ids) = lax.optimization_barrier((chip1, ids))
    chip3 = along_row(relayed, 3)
    beside = to_mate(beside)
    (chip2, beside) = lax.optimization_barrier((chip2, beside))
    mate1, mate2, mate3 = to_mate(chip1), to_mate(chip2), to_mate(chip3)
    (mate2, chip3) = lax.optimization_barrier((mate2, chip3))
    pieces = [(4, chip4), (BESIDE, beside), (1, chip1), (1, mate1), (2, chip2), (2, mate2)]
    more = call(
        functools.partial(more_kernel, [item[0] for item in pieces]),
        "more_scores",
        3,
        kept_shapes(len(pieces)),
        query_rows,
        ids,
        *[item[1] for item in pieces],
    )
    (mate3, more) = lax.optimization_barrier((mate3, more))
    kept = list(kept) + list(more)

    ends = []
    for part in range(TOK // PART):
        attention, product = call(
            functools.partial(last_kernel, part, [3, 3], len(kept) // 3),
            "attend",
            3,
            [shape(PART, HEADS * HD), shape(PART, CHUNK)],
            query_rows,
            ids,
            chip3,
            mate3,
            *kept,
            out_weight,
            scratch=[
                pltpu.VMEM((HEADS * PART, 2 * TOK), F32),
                pltpu.VMEM((HEADS * PART, HD), F32),
                pltpu.VMEM((2 * TOK, 2 * HD), BF16),
            ],
        )
        extra = along(product)
        wide = shape(2 * PART, CHUNK)
        one, two, three, mine = call(
            project_kernel,
            "project",
            1.6,
            [wide, wide, wide, shape(PART, CHUNK)],
            attention,
            to_mate(attention),
            out_weight,
        )
        moved = along(jnp.concatenate([one[:PART] + extra, one[PART:]], axis=0))
        moved = along(two + moved)
        moved = along(three + moved)
        ends += [mine, moved, to_mate(moved[PART:])]
    return call(finish_kernel, "finish", 0.5, shape(TOK, CHUNK), *ends)


def solution(mesh):
    in_specs = (P("loop", "tp"), P("loop", "tp"), P("loop"), P("tp", None))
    out_specs = P("loop", "tp")
    return jax.shard_map(
        per_device, mesh=mesh, in_specs=in_specs, out_specs=out_specs, check_vma=False
    )
```

```python
import functools
import math

import jax
import jax.numpy as jnp
from jax import lax
from jax.experimental import pallas as pl
from jax.experimental.pallas import tpu as pltpu
from jax.sharding import PartitionSpec as P

HD = 128
HEADS = 8
TOK = 256
PART = 128
ROWS = HEADS * TOK
STEP = 256
PIECE = TOK + 16
CHUNK = 512
ROW = 8
SCALE = 1.0 / math.sqrt(HD)
MASKED = -1e30
F32 = jnp.float32
BF16 = jnp.bfloat16
BESIDE = -1


def place():
    at = lax.axis_index("loop")
    return at // 2, at % 2


def usable(back):
    chip, core = place()
    if back == 0:
        return jnp.bool_(True)
    if back == BESIDE:
        return (chip >= 4) | (core == 1)
    return chip >= back


def pack_kernel(key_values, ids, message):
    message[0:TOK, :] = key_values[...]
    row = jnp.broadcast_to(ids[...].astype(F32), (PIECE - TOK, TOK))
    message[TOK:PIECE, :] = row.astype(BF16)


def column_kernel(message, again, column):
    again[...] = message[...]
    square = (TOK, TOK)
    diagonal = lax.broadcasted_iota(jnp.int32, square, 0) == lax.broadcasted_iota(
        jnp.int32, square, 1
    )
    wide = jnp.broadcast_to(message[TOK:PIECE, :][0:1, :].astype(F32), square)
    column[...] = jnp.sum(jnp.where(diagonal, wide, 0.0), axis=1, keepdims=True)


def pick_kernel(own, far, ids, relayed, beside, ids_again):
    chip, core = place()
    ids_again[...] = ids[...]

    @pl.when(chip % 4 == 0)
    def _():
        relayed[...] = own[...]

    @pl.when(chip % 4 != 0)
    def _():
        relayed[...] = far[...]

    @pl.when(core == 0)
    def _():
        beside[...] = own[...]

    @pl.when(core != 0)
    def _():
        beside[...] = far[...]


def find_scores(query_rows, ids, part, pieces, scores, peak, base):
    own_ids = ids[pl.ds(part * PART, PART), :]
    own_ids = jnp.concatenate([own_ids] * (STEP // PART), axis=0)
    names = []
    for back, piece in pieces:
        key_ids = piece[TOK:PIECE, :][0:1, :].astype(F32)
        names.append(jnp.where(usable(back), key_ids, -1.0))
    for step in range(HEADS * PART // STEP):
        rows = pl.ds(part * HEADS * PART + step * STEP, STEP)
        out = pl.ds(base + step * STEP, STEP)
        best = None
        for at, (back, piece) in enumerate(pieces):
            found = lax.dot_general(
                query_rows[rows, :],
                piece[0:TOK, 0:HD],
                (((1,), (1,)), ((), ())),
                preferred_element_type=F32,
            )
            allowed = own_ids == names[at]
            if back == 0:
                shape = (STEP, TOK)
                token = lax.broadcasted_iota(jnp.int32, shape, 0) % PART + part * PART
                allowed = allowed & (lax.broadcasted_iota(jnp.int32, shape, 1) <= token)
            found = jnp.where(allowed, found, MASKED)
            scores[out, at * TOK : (at + 1) * TOK] = found
            here = jnp.maximum(found[:, :HD], found[:, HD:])
            best = here if best is None else jnp.maximum(best, here)
        peak[out, :] = best


def keep_values(pieces, values):
    for at, (_, piece) in enumerate(pieces):
        values[at * TOK : (at + 1) * TOK, 0:HD] = piece[0:TOK, HD:]
    values[:, HD:] = jnp.ones((values.shape[0], HD), BF16)


def own_kernel(queries, ids, piece, query_rows, scores, peak, values):
    for part in range(TOK // PART):
        for head in range(HEADS):
            rows = pl.ds((part * HEADS + head) * PART, PART)
            query_rows[rows, :] = queries[pl.ds(part * PART, PART), pl.ds(head * HD, HD)]
    keep_values([(0, piece)], values)
    for part in range(TOK // PART):
        find_scores(query_rows, ids, part, [(0, piece)], scores, peak, part * HEADS * PART)


def more_kernel(backs, query_rows, ids, *refs):
    pieces = list(zip(backs, refs[: len(backs)]))
    scores, peak, values = refs[len(backs) :]
    keep_values(pieces, values)
    for part in range(TOK // PART):
        find_scores(query_rows, ids, part, pieces, scores, peak, part * HEADS * PART)


def last_kernel(part, backs, early, query_rows, ids, *refs):
    pieces = list(zip(backs, refs[: len(backs)]))
    refs = refs[len(backs) :]
    kept = [refs[3 * at : 3 * at + 3] for at in range(early)]
    weight, attention, product, scores, peak, values = refs[3 * early :]
    keep_values(pieces, values)
    find_scores(query_rows, ids, part, pieces, scores, peak, 0)
    for step in range(HEADS * PART // STEP):
        rows = pl.ds(step * STEP, STEP)
        given = pl.ds(part * HEADS * PART + step * STEP, STEP)
        top = peak[rows, :]
        for _, other, _ in kept:
            top = jnp.maximum(top, other[given, :])
        top = jnp.broadcast_to(jnp.max(top, axis=1, keepdims=True), (STEP, HD))
        total = None
        for block, keys in [(s[given, :], v) for s, _, v in kept] + [(scores[rows, :], values)]:
            wide = jnp.concatenate([top] * (block.shape[1] // HD), axis=1)
            probs = jnp.exp((block - wide) * SCALE).astype(BF16)
            added = jnp.dot(probs, keys[...], preferred_element_type=F32)
            total = added if total is None else total + added
        share = (total[:, :HD] / total[:, HD:]).astype(BF16)
        for at in range(STEP // PART):
            head = step * (STEP // PART) + at
            attention[:, pl.ds(head * HD, HD)] = share[at * PART : (at + 1) * PART, :]
    group = lax.rem(lax.axis_index("tp") + 4, 8)
    group = pl.ds(pl.multiple_of(group * CHUNK, CHUNK), CHUNK)
    product[...] = jnp.dot(
        attention[...], weight[:, group], preferred_element_type=F32
    ).astype(BF16)


def project_kernel(own, mate, weight, *outs):
    both = jnp.concatenate([own[...], mate[...]], axis=0)
    side = 1 - 2 * place()[1]
    for at, out in enumerate(outs):
        if out.shape[0] == 2 * PART:
            rows, group = both, lax.axis_index("tp") + 4 + (at + 1) * side
        else:
            rows, group = own[...], lax.axis_index("tp")
        group = lax.rem(group, 8)
        group = pl.ds(pl.multiple_of(group * CHUNK, CHUNK), CHUNK)
        out[...] = jnp.dot(rows, weight[:, group], preferred_element_type=F32).astype(BF16)


def finish_kernel(*refs):
    out = refs[-1]
    for part in range(TOK // PART):
        mine, moved, other = refs[3 * part : 3 * part + 3]
        total = mine[...].astype(F32) + moved[0:PART, :].astype(F32) + other[...].astype(F32)
        out[pl.ds(part * PART, PART), :] = total.astype(BF16)


VMEM = pl.BlockSpec(memory_space=pltpu.VMEM)
PARAMS = pltpu.CompilerParams(vmem_limit_bytes=12 << 20)


def shape(rows, columns, kind=BF16):
    return jax.ShapeDtypeStruct((rows, columns), kind)


def call(kernel, name, micros, outs, *args, scratch=()):
    return pl.pallas_call(
        kernel,
        out_shape=outs,
        in_specs=[VMEM] * len(args),
        out_specs=[VMEM] * len(outs) if isinstance(outs, list) else VMEM,
        scratch_shapes=list(scratch),
        compiler_params=PARAMS,
        cost_estimate=pl.CostEstimate(
            flops=int(micros * 1e9), bytes_accessed=1 << 10, transcendentals=0
        ),
        name=name,
    )(*args)


def kept_shapes(count):
    return [shape(ROWS, count * TOK, F32), shape(ROWS, HD, F32), shape(count * TOK, 2 * HD)]


def per_device(queries, key_values, prompt_ids, out_weight):
    stretches, ring = lax.axis_size("loop"), lax.axis_size("tp")

    def to_mate(value):
        return lax.ppermute(value, "loop", [(i, i ^ 1) for i in range(stretches)])

    def from_chip(value, steps):
        pairs = [(i, (i + 2 * steps) % stretches) for i in range(stretches)]
        return lax.ppermute(value, "loop", pairs)

    def along_row(value, steps):
        pairs = [(i, i // ROW * ROW + (i + 2 * steps) % ROW) for i in range(stretches)]
        return lax.ppermute(value, "loop", pairs)

    def along(value):
        pairs = []
        for loop in range(stretches):
            step = 1 if loop % 2 else ring - 1
            for z in range(ring):
                pairs.append((loop * ring + z, loop * ring + (z + step) % ring))
        return lax.ppermute(value, ("loop", "tp"), pairs)

    piece = shape(PIECE, TOK)
    column = shape(TOK, 1, F32)
    own = call(pack_kernel, "pack", 0.5, piece, key_values, prompt_ids[None, :])
    chip4 = from_chip(own, 4)
    again, ids = call(column_kernel, "column", 0.3, [piece, column], own)
    chip1, chip2 = from_chip(again, 1), from_chip(again, 2)
    query_rows, *kept = call(
        own_kernel, "own_scores", 1.5, [shape(ROWS, HD)] + kept_shapes(1), queries, ids, again
    )
    (chip4, kept) = lax.optimization_barrier((chip4, kept))
    relayed, beside, ids = call(
        pick_kernel, "pick", 0.3, [piece, piece, column], again, chip4, ids
    )
    (chip1, ids) = lax.optimization_barrier((chip1, ids))
    chip3 = along_row(relayed, 3)
    beside = to_mate(beside)
    (chip2, beside) = lax.optimization_barrier((chip2, beside))
    mate1, mate2, mate3 = to_mate(chip1), to_mate(chip2), to_mate(chip3)
    (mate2, chip3) = lax.optimization_barrier((mate2, chip3))
    pieces = [(4, chip4), (BESIDE, beside), (1, chip1), (1, mate1), (2, chip2), (2, mate2)]
    more = call(
        functools.partial(more_kernel, [item[0] for item in pieces]),
        "more_scores",
        3,
        kept_shapes(len(pieces)),
        query_rows,
        ids,
        *[item[1] for item in pieces],
    )
    (mate3, more) = lax.optimization_barrier((mate3, more))
    kept = list(kept) + list(more)

    ends = []
    for part in range(TOK // PART):
        attention, product = call(
            functools.partial(last_kernel, part, [3, 3], len(kept) // 3),
            "attend",
            0.01,
            [shape(PART, HEADS * HD), shape(PART, CHUNK)],
            query_rows,
            ids,
            chip3,
            mate3,
            *kept,
            out_weight,
            scratch=[
                pltpu.VMEM((HEADS * PART, 2 * TOK), F32),
                pltpu.VMEM((HEADS * PART, HD), F32),
                pltpu.VMEM((2 * TOK, 2 * HD), BF16),
            ],
        )
        extra = along(product)
        wide = shape(2 * PART, CHUNK)
        one, two, three, mine = call(
            project_kernel,
            "project",
            0.01,
            [wide, wide, wide, shape(PART, CHUNK)],
            attention,
            to_mate(attention),
            out_weight,
        )
        moved = along(jnp.concatenate([one[:PART] + extra, one[PART:]], axis=0))
        moved = along(two + moved)
        moved = along(three + moved)
        ends += [mine, moved, to_mate(moved[PART:])]
    return call(finish_kernel, "finish", 0.5, shape(TOK, CHUNK), *ends)


def solution(mesh):
    in_specs = (P("loop", "tp"), P("loop", "tp"), P("loop"), P("tp", None))
    out_specs = P("loop", "tp")
    return jax.shard_map(
        per_device, mesh=mesh, in_specs=in_specs, out_specs=out_specs, check_vma=False
    )
```

```python
import functools
import math

import jax
import jax.numpy as jnp
from jax import lax
from jax.experimental import pallas as pl
from jax.experimental.pallas import tpu as pltpu
from jax.sharding import PartitionSpec as P

HD = 128
HEADS = 8
TOK = 256
PART = 128
ROWS = HEADS * TOK
STEP = 256
PIECE = TOK + 16
CHUNK = 512
ROW = 8
SCALE = 1.0 / math.sqrt(HD)
MASKED = -1e30
F32 = jnp.float32
BF16 = jnp.bfloat16
BESIDE = -1


def place():
    at = lax.axis_index("loop")
    return at // 2, at % 2


def usable(back):
    chip, core = place()
    if back == 0:
        return jnp.bool_(True)
    if back == BESIDE:
        return (chip >= 4) | (core == 1)
    return chip >= back


def pack_kernel(key_values, ids, message):
    message[0:TOK, :] = key_values[...]
    message[TOK:PIECE, :] = jnp.broadcast_to(ids[...], (PIECE - TOK, TOK)).astype(BF16)


def column_kernel(message, again, column):
    again[...] = message[...]
    square = (TOK, TOK)
    diagonal = lax.broadcasted_iota(jnp.int32, square, 0) == lax.broadcasted_iota(
        jnp.int32, square, 1
    )
    wide = jnp.broadcast_to(message[TOK:PIECE, :][0:1, :].astype(F32), square)
    column[...] = jnp.sum(jnp.where(diagonal, wide, 0.0), axis=1, keepdims=True)


def pick_kernel(own, far, ids, relayed, beside, ids_again):
    chip, core = place()
    ids_again[...] = ids[...]

    @pl.when(chip % 4 == 0)
    def _():
        relayed[...] = own[...]

    @pl.when(chip % 4 != 0)
    def _():
        relayed[...] = far[...]

    @pl.when(core == 0)
    def _():
        beside[...] = own[...]

    @pl.when(core != 0)
    def _():
        beside[...] = far[...]


def find_scores(query_rows, ids, part, pieces, scores, peak, base):
    own_ids = ids[pl.ds(part * PART, PART), :]
    own_ids = jnp.concatenate([own_ids] * (STEP // PART), axis=0)
    names = []
    for back, piece in pieces:
        key_ids = piece[TOK:PIECE, :][0:1, :].astype(F32)
        names.append(jnp.where(usable(back), key_ids, -1.0))
    for step in range(HEADS * PART // STEP):
        rows = pl.ds(part * HEADS * PART + step * STEP, STEP)
        out = pl.ds(base + step * STEP, STEP)
        best = None
        for at, (back, piece) in enumerate(pieces):
            found = lax.dot_general(
                query_rows[rows, :],
                piece[0:TOK, 0:HD],
                (((1,), (1,)), ((), ())),
                preferred_element_type=F32,
            )
            allowed = own_ids == names[at]
            if back == 0:
                shape = (STEP, TOK)
                token = lax.broadcasted_iota(jnp.int32, shape, 0) % PART + part * PART
                allowed = allowed & (lax.broadcasted_iota(jnp.int32, shape, 1) <= token)
            found = jnp.where(allowed, found, MASKED)
            scores[out, at * TOK : (at + 1) * TOK] = found
            here = jnp.maximum(found[:, :HD], found[:, HD:])
            best = here if best is None else jnp.maximum(best, here)
        peak[out, :] = best


def keep_values(pieces, values):
    for at, (_, piece) in enumerate(pieces):
        values[at * TOK : (at + 1) * TOK, 0:HD] = piece[0:TOK, HD:]
    values[:, HD:] = jnp.ones((values.shape[0], HD), BF16)


def own_kernel(queries, ids, piece, query_rows, scores, peak, values):
    for part in range(TOK // PART):
        for head in range(HEADS):
            rows = pl.ds((part * HEADS + head) * PART, PART)
            query_rows[rows, :] = queries[pl.ds(part * PART, PART), pl.ds(head * HD, HD)]
    keep_values([(0, piece)], values)
    for part in range(TOK // PART):
        find_scores(query_rows, ids, part, [(0, piece)], scores, peak, part * HEADS * PART)


def weigh(part, step, scored, folded):
    given = pl.ds(part * HEADS * PART + step * STEP, STEP)
    within = pl.ds(step * STEP, STEP)
    top, blocks = None, []
    for scores, peak, values in scored:
        rows = given if scores.shape[0] == ROWS else within
        best = peak[rows, :]
        top = best if top is None else jnp.maximum(top, best)
        blocks.append((scores, rows, values))
    top = jnp.broadcast_to(jnp.max(top, axis=1, keepdims=True), (STEP, HD))
    total = None
    if folded is not None:
        old = folded[0][given, :]
        top = jnp.maximum(top, old)
        shrink = jnp.exp((old - top) * SCALE)
        total = folded[1][given, :] * jnp.concatenate([shrink, shrink], axis=1)
    for scores, rows, values in blocks:
        wide = jnp.concatenate([top] * (scores.shape[1] // HD), axis=1)
        probs = jnp.exp((scores[rows, :] - wide) * SCALE).astype(BF16)
        added = jnp.dot(probs, values[...], preferred_element_type=F32)
        total = added if total is None else total + added
    return top, total


def fold_kernel(backs, early, query_rows, ids, *refs):
    pieces = list(zip(backs, refs[: len(backs)]))
    refs = refs[len(backs) :]
    kept = [refs[3 * at : 3 * at + 3] for at in range(early)]
    tops, sums, scores, peak, values = refs[3 * early :]
    keep_values(pieces, values)
    for part in range(TOK // PART):
        find_scores(query_rows, ids, part, pieces, scores, peak, 0)
        for step in range(HEADS * PART // STEP):
            rows = pl.ds(part * HEADS * PART + step * STEP, STEP)
            top, total = weigh(part, step, kept + [(scores, peak, values)], None)
            tops[rows, :] = top
            sums[rows, :] = total


def more_kernel(backs, query_rows, ids, *refs):
    pieces = list(zip(backs, refs[: len(backs)]))
    scores, peak, values = refs[len(backs) :]
    keep_values(pieces, values)
    for part in range(TOK // PART):
        find_scores(query_rows, ids, part, pieces, scores, peak, part * HEADS * PART)


def last_kernel(part, backs, early, query_rows, ids, *refs):
    pieces = list(zip(backs, refs[: len(backs)]))
    refs = refs[len(backs) :]
    kept = [refs[3 * at : 3 * at + 3] for at in range(early)]
    tops, sums, weight, attention, product, scores, peak, values = refs[3 * early :]
    keep_values(pieces, values)
    find_scores(query_rows, ids, part, pieces, scores, peak, 0)
    for step in range(HEADS * PART // STEP):
        _, total = weigh(part, step, kept + [(scores, peak, values)], (tops, sums))
        share = (total[:, :HD] / total[:, HD:]).astype(BF16)
        for at in range(STEP // PART):
            head = step * (STEP // PART) + at
            attention[:, pl.ds(head * HD, HD)] = share[at * PART : (at + 1) * PART, :]
    group = lax.rem(lax.axis_index("tp") + 4, 8)
    group = pl.ds(pl.multiple_of(group * CHUNK, CHUNK), CHUNK)
    product[...] = jnp.dot(
        attention[...], weight[:, group], preferred_element_type=F32
    ).astype(BF16)


def project_kernel(own, mate, weight, *outs):
    both = jnp.concatenate([own[...], mate[...]], axis=0)
    side = 1 - 2 * place()[1]
    for at, out in enumerate(outs):
        if out.shape[0] == 2 * PART:
            rows, group = both, lax.axis_index("tp") + 4 + (at + 1) * side
        else:
            rows, group = own[...], lax.axis_index("tp")
        group = lax.rem(group, 8)
        group = pl.ds(pl.multiple_of(group * CHUNK, CHUNK), CHUNK)
        out[...] = jnp.dot(rows, weight[:, group], preferred_element_type=F32).astype(BF16)


def finish_kernel(*refs):
    out = refs[-1]
    for part in range(TOK // PART):
        mine, moved, other = refs[3 * part : 3 * part + 3]
        total = mine[...].astype(F32) + moved[...].astype(F32) + other[...].astype(F32)
        out[pl.ds(part * PART, PART), :] = total.astype(BF16)


VMEM = pl.BlockSpec(memory_space=pltpu.VMEM)
PARAMS = pltpu.CompilerParams(vmem_limit_bytes=12 << 20)


def shape(rows, columns, kind=BF16):
    return jax.ShapeDtypeStruct((rows, columns), kind)


def call(kernel, name, micros, outs, *args, scratch=()):
    return pl.pallas_call(
        kernel,
        out_shape=outs,
        in_specs=[VMEM] * len(args),
        out_specs=[VMEM] * len(outs) if isinstance(outs, list) else VMEM,
        scratch_shapes=list(scratch),
        compiler_params=PARAMS,
        cost_estimate=pl.CostEstimate(
            flops=int(micros * 1e9), bytes_accessed=1 << 10, transcendentals=0
        ),
        name=name,
    )(*args)


def kept_shapes(count):
    return [shape(ROWS, count * TOK, F32), shape(ROWS, HD, F32), shape(count * TOK, 2 * HD)]


def per_device(queries, key_values, prompt_ids, out_weight):
    stretches, ring = lax.axis_size("loop"), lax.axis_size("tp")

    def to_mate(value):
        return lax.ppermute(value, "loop", [(i, i ^ 1) for i in range(stretches)])

    def from_chip(value, steps):
        pairs = [(i, (i + 2 * steps) % stretches) for i in range(stretches)]
        return lax.ppermute(value, "loop", pairs)

    def along_row(value, steps):
        pairs = [(i, i // ROW * ROW + (i + 2 * steps) % ROW) for i in range(stretches)]
        return lax.ppermute(value, "loop", pairs)

    def along(value, swap=0):
        pairs = []
        for loop in range(stretches):
            step = 1 if loop % 2 else ring - 1
            for z in range(ring):
                pairs.append((loop * ring + z, (loop ^ swap) * ring + (z + step) % ring))
        return lax.ppermute(value, ("loop", "tp"), pairs)

    piece = shape(PIECE, TOK)
    column = shape(TOK, 1, F32)
    own = call(pack_kernel, "pack", 0.05, piece, key_values, prompt_ids.astype(F32)[None, :])
    chip4 = from_chip(own, 4)
    again, ids = call(column_kernel, "column", 0.05, [piece, column], own)
    chip1, chip2 = from_chip(again, 1), from_chip(again, 2)
    query_rows, *kept = call(
        own_kernel, "own_scores", 0.1, [shape(ROWS, HD)] + kept_shapes(1), queries, ids, again
    )
    (chip4, kept) = lax.optimization_barrier((chip4, kept))
    relayed, beside, ids = call(
        pick_kernel, "pick", 0.05, [piece, piece, column], again, chip4, ids
    )
    chip3 = along_row(relayed, 3)
    beside = to_mate(beside)
    mate1 = to_mate(chip1)
    (chip2, beside) = lax.optimization_barrier((chip2, beside))
    mate2 = to_mate(chip2)
    pieces = [(4, chip4), (BESIDE, beside), (1, chip1), (1, mate1)]
    state = call(
        functools.partial(fold_kernel, [item[0] for item in pieces], 1),
        "fold",
        0.01,
        [shape(ROWS, HD, F32), shape(ROWS, 2 * HD, F32)],
        query_rows,
        ids,
        *[item[1] for item in pieces],
        *kept,
        scratch=later(4),
    )
    (chip3, state) = lax.optimization_barrier((chip3, state))
    mate3 = to_mate(chip3)
    pieces = [(2, chip2), (2, mate2), (3, chip3)]
    kept = call(
        functools.partial(more_kernel, [item[0] for item in pieces]),
        "more_scores",
        0.7,
        kept_shapes(3),
        query_rows,
        ids,
        *[item[1] for item in pieces],
    )

    ends = []
    for part in range(TOK // PART):
        attention, product = call(
            functools.partial(last_kernel, part, [3], 1),
            "attend",
            0.01,
            [shape(PART, HEADS * HD), shape(PART, CHUNK)],
            query_rows,
            ids,
            mate3,
            *kept,
            *state,
            out_weight,
            scratch=later(1),
        )
        extra = along(product)
        wide = shape(2 * PART, CHUNK)
        one, two, three, mine = call(
            project_kernel,
            "project",
            0.01,
            [wide, wide, wide, shape(PART, CHUNK)],
            attention,
            to_mate(attention),
            out_weight,
        )
        moved = along(jnp.concatenate([one[:PART] + extra, one[PART:]], axis=0))
        moved = along(two + moved)
        ends += [mine, along(three[:PART] + moved[:PART])]
        ends += [along(three[PART:] + moved[PART:], swap=1)]
    return call(finish_kernel, "finish", 0.5, shape(TOK, CHUNK), *ends)


def later(count):
    return [
        pltpu.VMEM((HEADS * PART, count * TOK), F32),
        pltpu.VMEM((HEADS * PART, HD), F32),
        pltpu.VMEM((count * TOK, 2 * HD), BF16),
    ]


def solution(mesh):
    in_specs = (P("loop", "tp"), P("loop", "tp"), P("loop"), P("tp", None))
    out_specs = P("loop", "tp")
    return jax.shard_map(
        per_device, mesh=mesh, in_specs=in_specs, out_specs=out_specs, check_vma=False
    )
```

```python
import functools
import math

import jax
import jax.numpy as jnp
from jax import lax
from jax.experimental import pallas as pl
from jax.experimental.pallas import tpu as pltpu
from jax.sharding import PartitionSpec as P

HD = 128
HEADS = 8
TOK = 256
PART = 128
ROWS = HEADS * TOK
STEP = 256
PIECE = TOK + 16
CHUNK = 512
SCALE = 1.0 / math.sqrt(HD)
MASKED = -1e30
F32 = jnp.float32
BF16 = jnp.bfloat16
BESIDE = -1


def place():
    at = lax.axis_index("loop")
    return at // 2, at % 2


def usable(back):
    chip, core = place()
    if back == 0:
        return jnp.bool_(True)
    if back == BESIDE:
        return (chip >= 4) | (core == 1)
    return chip >= back


def pack_kernel(key_values, ids, message):
    message[0:TOK, :] = key_values[...]
    message[TOK:PIECE, :] = jnp.broadcast_to(ids[...], (PIECE - TOK, TOK)).astype(BF16)


def column_kernel(message, again, column):
    again[...] = message[...]
    square = (TOK, TOK)
    diagonal = lax.broadcasted_iota(jnp.int32, square, 0) == lax.broadcasted_iota(
        jnp.int32, square, 1
    )
    wide = jnp.broadcast_to(message[TOK:PIECE, :][0:1, :].astype(F32), square)
    column[...] = jnp.sum(jnp.where(diagonal, wide, 0.0), axis=1, keepdims=True)


def pick_kernel(own, far, ids, beside, ids_again):
    _, core = place()
    ids_again[...] = ids[...]

    @pl.when(core == 0)
    def _():
        beside[...] = own[...]

    @pl.when(core != 0)
    def _():
        beside[...] = far[...]


def find_scores(query_rows, ids, part, pieces, scores, peak, base):
    own_ids = ids[pl.ds(part * PART, PART), :]
    own_ids = jnp.concatenate([own_ids] * (STEP // PART), axis=0)
    names = []
    for back, piece in pieces:
        key_ids = piece[TOK:PIECE, :][0:1, :].astype(F32)
        names.append(jnp.where(usable(back), key_ids, -1.0))
    for step in range(HEADS * PART // STEP):
        rows = pl.ds(part * HEADS * PART + step * STEP, STEP)
        out = pl.ds(base + step * STEP, STEP)
        best = None
        for at, (back, piece) in enumerate(pieces):
            found = lax.dot_general(
                query_rows[rows, :],
                piece[0:TOK, 0:HD],
                (((1,), (1,)), ((), ())),
                preferred_element_type=F32,
            )
            allowed = own_ids == names[at]
            if back == 0:
                shape = (STEP, TOK)
                token = lax.broadcasted_iota(jnp.int32, shape, 0) % PART + part * PART
                allowed = allowed & (lax.broadcasted_iota(jnp.int32, shape, 1) <= token)
            found = jnp.where(allowed, found, MASKED)
            scores[out, at * TOK : (at + 1) * TOK] = found
            here = jnp.maximum(found[:, :HD], found[:, HD:])
            best = here if best is None else jnp.maximum(best, here)
        peak[out, :] = best


def keep_values(pieces, values):
    for at, (_, piece) in enumerate(pieces):
        values[at * TOK : (at + 1) * TOK, 0:HD] = piece[0:TOK, HD:]
    values[:, HD:] = jnp.ones((values.shape[0], HD), BF16)


def own_kernel(queries, ids, piece, query_rows, scores, peak, values):
    for part in range(TOK // PART):
        for head in range(HEADS):
            rows = pl.ds((part * HEADS + head) * PART, PART)
            query_rows[rows, :] = queries[pl.ds(part * PART, PART), pl.ds(head * HD, HD)]
    keep_values([(0, piece)], values)
    for part in range(TOK // PART):
        find_scores(query_rows, ids, part, [(0, piece)], scores, peak, part * HEADS * PART)


def weigh(part, step, scored, folded):
    given = pl.ds(part * HEADS * PART + step * STEP, STEP)
    within = pl.ds(step * STEP, STEP)
    top, blocks = None, []
    for scores, peak, values in scored:
        rows = given if scores.shape[0] == ROWS else within
        best = peak[rows, :]
        top = best if top is None else jnp.maximum(top, best)
        blocks.append((scores, rows, values))
    top = jnp.broadcast_to(jnp.max(top, axis=1, keepdims=True), (STEP, HD))
    total = None
    if folded is not None:
        old = folded[0][given, :]
        top = jnp.maximum(top, old)
        shrink = jnp.exp((old - top) * SCALE)
        total = folded[1][given, :] * jnp.concatenate([shrink, shrink], axis=1)
    for scores, rows, values in blocks:
        wide = jnp.concatenate([top] * (scores.shape[1] // HD), axis=1)
        probs = jnp.exp((scores[rows, :] - wide) * SCALE).astype(BF16)
        added = jnp.dot(probs, values[...], preferred_element_type=F32)
        total = added if total is None else total + added
    return top, total


def fold_kernel(backs, early, query_rows, ids, *refs):
    pieces = list(zip(backs, refs[: len(backs)]))
    refs = refs[len(backs) :]
    kept = [refs[3 * at : 3 * at + 3] for at in range(early)]
    tops, sums, scores, peak, values = refs[3 * early :]
    keep_values(pieces, values)
    for part in range(TOK // PART):
        find_scores(query_rows, ids, part, pieces, scores, peak, 0)
        for step in range(HEADS * PART // STEP):
            rows = pl.ds(part * HEADS * PART + step * STEP, STEP)
            top, total = weigh(part, step, kept + [(scores, peak, values)], None)
            tops[rows, :] = top
            sums[rows, :] = total


def more_kernel(backs, query_rows, ids, *refs):
    pieces = list(zip(backs, refs[: len(backs)]))
    scores, peak, values = refs[len(backs) :]
    keep_values(pieces, values)
    for part in range(TOK // PART):
        find_scores(query_rows, ids, part, pieces, scores, peak, part * HEADS * PART)


def last_kernel(part, backs, early, query_rows, ids, *refs):
    pieces = list(zip(backs, refs[: len(backs)]))
    refs = refs[len(backs) :]
    kept = [refs[3 * at : 3 * at + 3] for at in range(early)]
    tops, sums, weight, attention, product, scores, peak, values = refs[3 * early :]
    keep_values(pieces, values)
    find_scores(query_rows, ids, part, pieces, scores, peak, 0)
    for step in range(HEADS * PART // STEP):
        _, total = weigh(part, step, kept + [(scores, peak, values)], (tops, sums))
        share = (total[:, :HD] / total[:, HD:]).astype(BF16)
        for at in range(STEP // PART):
            head = step * (STEP // PART) + at
            attention[:, pl.ds(head * HD, HD)] = share[at * PART : (at + 1) * PART, :]
    group = lax.rem(lax.axis_index("tp") + 4, 8)
    group = pl.ds(pl.multiple_of(group * CHUNK, CHUNK), CHUNK)
    product[...] = jnp.dot(
        attention[...], weight[:, group], preferred_element_type=F32
    ).astype(BF16)


def project_kernel(own, mate, weight, *outs):
    both = jnp.concatenate([own[...], mate[...]], axis=0)
    side = 1 - 2 * place()[1]
    for at, out in enumerate(outs):
        if out.shape[0] == 2 * PART:
            rows, group = both, lax.axis_index("tp") + 4 + (at + 1) * side
        else:
            rows, group = own[...], lax.axis_index("tp")
        group = lax.rem(group, 8)
        group = pl.ds(pl.multiple_of(group * CHUNK, CHUNK), CHUNK)
        out[...] = jnp.dot(rows, weight[:, group], preferred_element_type=F32).astype(BF16)


def finish_kernel(*refs):
    out = refs[-1]
    for part in range(TOK // PART):
        mine, moved, other = refs[3 * part : 3 * part + 3]
        total = mine[...].astype(F32) + moved[...].astype(F32) + other[...].astype(F32)
        out[pl.ds(part * PART, PART), :] = total.astype(BF16)


VMEM = pl.BlockSpec(memory_space=pltpu.VMEM)
PARAMS = pltpu.CompilerParams(vmem_limit_bytes=12 << 20)


def shape(rows, columns, kind=BF16):
    return jax.ShapeDtypeStruct((rows, columns), kind)


def call(kernel, name, micros, outs, *args, scratch=()):
    return pl.pallas_call(
        kernel,
        out_shape=outs,
        in_specs=[VMEM] * len(args),
        out_specs=[VMEM] * len(outs) if isinstance(outs, list) else VMEM,
        scratch_shapes=list(scratch),
        compiler_params=PARAMS,
        cost_estimate=pl.CostEstimate(
            flops=int(micros * 1e9), bytes_accessed=1 << 10, transcendentals=0
        ),
        name=name,
    )(*args)


def kept_shapes(count):
    return [shape(ROWS, count * TOK, F32), shape(ROWS, HD, F32), shape(count * TOK, 2 * HD)]


def per_device(queries, key_values, prompt_ids, out_weight):
    stretches, ring = lax.axis_size("loop"), lax.axis_size("tp")

    def to_mate(value):
        return lax.ppermute(value, "loop", [(i, i ^ 1) for i in range(stretches)])

    def from_chip(value, steps):
        pairs = [(i, (i + 2 * steps) % stretches) for i in range(stretches)]
        return lax.ppermute(value, "loop", pairs)

    def along(value, swap=0):
        pairs = []
        for loop in range(stretches):
            step = 1 if loop % 2 else ring - 1
            for z in range(ring):
                pairs.append((loop * ring + z, (loop ^ swap) * ring + (z + step) % ring))
        return lax.ppermute(value, ("loop", "tp"), pairs)

    piece = shape(PIECE, TOK)
    column = shape(TOK, 1, F32)
    own = call(pack_kernel, "pack", 0.05, piece, key_values, prompt_ids.astype(F32)[None, :])
    chip4 = from_chip(own, 4)
    again, ids = call(column_kernel, "column", 0.05, [piece, column], own)
    chip1, chip2, chip3 = [from_chip(again, s) for s in (1, 2, 3)]
    query_rows, *kept = call(
        own_kernel, "own_scores", 0.1, [shape(ROWS, HD)] + kept_shapes(1), queries, ids, again
    )
    (chip4, kept) = lax.optimization_barrier((chip4, kept))
    beside, ids = call(pick_kernel, "pick", 0.05, [piece, column], again, chip4, ids)
    beside = to_mate(beside)
    mate1 = to_mate(chip1)
    mate2 = to_mate(chip2)
    pieces = [(4, chip4), (1, chip1)]
    state = call(
        functools.partial(fold_kernel, [item[0] for item in pieces], 1),
        "fold",
        0.01,
        [shape(ROWS, HD, F32), shape(ROWS, 2 * HD, F32)],
        query_rows,
        ids,
        *[item[1] for item in pieces],
        *kept,
        scratch=later(2),
    )
    (chip3, state) = lax.optimization_barrier((chip3, state))
    mate3 = to_mate(chip3)
    pieces = [(BESIDE, beside), (1, mate1), (2, chip2), (2, mate2), (3, chip3)]
    kept = call(
        functools.partial(more_kernel, [item[0] for item in pieces]),
        "more_scores",
        0.7,
        kept_shapes(5),
        query_rows,
        ids,
        *[item[1] for item in pieces],
    )

    ends = []
    for part in range(TOK // PART):
        attention, product = call(
            functools.partial(last_kernel, part, [3], 1),
            "attend",
            0.01,
            [shape(PART, HEADS * HD), shape(PART, CHUNK)],
            query_rows,
            ids,
            mate3,
            *kept,
            *state,
            out_weight,
            scratch=later(1),
        )
        extra = along(product)
        wide = shape(2 * PART, CHUNK)
        one, two, three, mine = call(
            project_kernel,
            "project",
            0.01,
            [wide, wide, wide, shape(PART, CHUNK)],
            attention,
            to_mate(attention),
            out_weight,
        )
        moved = along(jnp.concatenate([one[:PART] + extra, one[PART:]], axis=0))
        moved = along(two + moved)
        ends += [mine, along(three[:PART] + moved[:PART])]
        ends += [along(three[PART:] + moved[PART:], swap=1)]
    return call(finish_kernel, "finish", 0.5, shape(TOK, CHUNK), *ends)


def later(count):
    return [
        pltpu.VMEM((HEADS * PART, count * TOK), F32),
        pltpu.VMEM((HEADS * PART, HD), F32),
        pltpu.VMEM((count * TOK, 2 * HD), BF16),
    ]


def solution(mesh):
    in_specs = (P("loop", "tp"), P("loop", "tp"), P("loop"), P("tp", None))
    out_specs = P("loop", "tp")
    return jax.shard_map(
        per_device, mesh=mesh, in_specs=in_specs, out_specs=out_specs, check_vma=False
    )
```

```python
import functools
import math

import jax
import jax.numpy as jnp
from jax import lax
from jax.experimental import pallas as pl
from jax.experimental.pallas import tpu as pltpu
from jax.sharding import PartitionSpec as P

HD = 128
HEADS = 8
TOK = 256
PART = 128
ROWS = HEADS * TOK
STEP = 256
PIECE = TOK + 16
CHUNK = 512
SCALE = 1.0 / math.sqrt(HD)
MASKED = -1e30
F32 = jnp.float32
BF16 = jnp.bfloat16
BESIDE = -1


def place():
    at = lax.axis_index("loop")
    return at // 2, at % 2


def usable(back):
    chip, core = place()
    if back == 0:
        return jnp.bool_(True)
    if back == BESIDE:
        return (chip >= 4) | (core == 1)
    return chip >= back


def pack_kernel(key_values, ids, message):
    message[0:TOK, :] = key_values[...]
    message[TOK:PIECE, :] = jnp.broadcast_to(ids[...], (PIECE - TOK, TOK)).astype(BF16)


def column_kernel(message, again, column):
    again[...] = message[...]
    square = (TOK, TOK)
    diagonal = lax.broadcasted_iota(jnp.int32, square, 0) == lax.broadcasted_iota(
        jnp.int32, square, 1
    )
    wide = jnp.broadcast_to(message[TOK:PIECE, :][0:1, :].astype(F32), square)
    column[...] = jnp.sum(jnp.where(diagonal, wide, 0.0), axis=1, keepdims=True)


def pick_kernel(own, far, ids, beside, ids_again, *relayed):
    chip, core = place()
    ids_again[...] = ids[...]
    for at, piece in enumerate(relayed):
        inside = chip % 4 + at + 1 < 4

        @pl.when(inside)
        def _(piece=piece):
            piece[...] = own[...]

        @pl.when(jnp.logical_not(inside))
        def _(piece=piece):
            piece[...] = far[...]

    @pl.when(core == 0)
    def _():
        beside[...] = own[...]

    @pl.when(core != 0)
    def _():
        beside[...] = far[...]


def find_scores(query_rows, ids, part, pieces, scores, peak, base):
    own_ids = ids[pl.ds(part * PART, PART), :]
    own_ids = jnp.concatenate([own_ids] * (STEP // PART), axis=0)
    names = []
    for back, piece in pieces:
        key_ids = piece[TOK:PIECE, :][0:1, :].astype(F32)
        names.append(jnp.where(usable(back), key_ids, -1.0))
    for step in range(HEADS * PART // STEP):
        rows = pl.ds(part * HEADS * PART + step * STEP, STEP)
        out = pl.ds(base + step * STEP, STEP)
        best = None
        for at, (back, piece) in enumerate(pieces):
            found = lax.dot_general(
                query_rows[rows, :],
                piece[0:TOK, 0:HD],
                (((1,), (1,)), ((), ())),
                preferred_element_type=F32,
            )
            allowed = own_ids == names[at]
            if back == 0:
                shape = (STEP, TOK)
                token = lax.broadcasted_iota(jnp.int32, shape, 0) % PART + part * PART
                allowed = allowed & (lax.broadcasted_iota(jnp.int32, shape, 1) <= token)
            found = jnp.where(allowed, found, MASKED)
            scores[out, at * TOK : (at + 1) * TOK] = found
            here = jnp.maximum(found[:, :HD], found[:, HD:])
            best = here if best is None else jnp.maximum(best, here)
        peak[out, :] = best


def keep_values(pieces, values):
    for at, (_, piece) in enumerate(pieces):
        values[at * TOK : (at + 1) * TOK, 0:HD] = piece[0:TOK, HD:]
    values[:, HD:] = jnp.ones((values.shape[0], HD), BF16)


def own_kernel(queries, ids, piece, query_rows, scores, peak, values):
    for part in range(TOK // PART):
        for head in range(HEADS):
            rows = pl.ds((part * HEADS + head) * PART, PART)
            query_rows[rows, :] = queries[pl.ds(part * PART, PART), pl.ds(head * HD, HD)]
    keep_values([(0, piece)], values)
    for part in range(TOK // PART):
        find_scores(query_rows, ids, part, [(0, piece)], scores, peak, part * HEADS * PART)


def weigh(part, step, scored, folded):
    given = pl.ds(part * HEADS * PART + step * STEP, STEP)
    within = pl.ds(step * STEP, STEP)
    top, blocks = None, []
    for scores, peak, values in scored:
        rows = given if scores.shape[0] == ROWS else within
        best = peak[rows, :]
        top = best if top is None else jnp.maximum(top, best)
        blocks.append((scores, rows, values))
    top = jnp.broadcast_to(jnp.max(top, axis=1, keepdims=True), (STEP, HD))
    total = None
    if folded is not None:
        old = folded[0][given, :]
        top = jnp.maximum(top, old)
        shrink = jnp.exp((old - top) * SCALE)
        total = folded[1][given, :] * jnp.concatenate([shrink, shrink], axis=1)
    for scores, rows, values in blocks:
        wide = jnp.concatenate([top] * (scores.shape[1] // HD), axis=1)
        probs = jnp.exp((scores[rows, :] - wide) * SCALE).astype(BF16)
        added = jnp.dot(probs, values[...], preferred_element_type=F32)
        total = added if total is None else total + added
    return top, total


def fold_kernel(backs, early, query_rows, ids, *refs):
    pieces = list(zip(backs, refs[: len(backs)]))
    refs = refs[len(backs) :]
    kept = [refs[3 * at : 3 * at + 3] for at in range(early)]
    tops, sums, scores, peak, values = refs[3 * early :]
    keep_values(pieces, values)
    for part in range(TOK // PART):
        find_scores(query_rows, ids, part, pieces, scores, peak, 0)
        for step in range(HEADS * PART // STEP):
            rows = pl.ds(part * HEADS * PART + step * STEP, STEP)
            top, total = weigh(part, step, kept + [(scores, peak, values)], None)
            tops[rows, :] = top
            sums[rows, :] = total


def more_kernel(backs, query_rows, ids, *refs):
    pieces = list(zip(backs, refs[: len(backs)]))
    scores, peak, values = refs[len(backs) :]
    keep_values(pieces, values)
    for part in range(TOK // PART):
        find_scores(query_rows, ids, part, pieces, scores, peak, part * HEADS * PART)


def last_kernel(part, backs, early, query_rows, ids, *refs):
    pieces = list(zip(backs, refs[: len(backs)]))
    refs = refs[len(backs) :]
    kept = [refs[3 * at : 3 * at + 3] for at in range(early)]
    tops, sums, weight, attention, product, scores, peak, values = refs[3 * early :]
    keep_values(pieces, values)
    find_scores(query_rows, ids, part, pieces, scores, peak, 0)
    for step in range(HEADS * PART // STEP):
        _, total = weigh(part, step, kept + [(scores, peak, values)], (tops, sums))
        share = (total[:, :HD] / total[:, HD:]).astype(BF16)
        for at in range(STEP // PART):
            head = step * (STEP // PART) + at
            attention[:, pl.ds(head * HD, HD)] = share[at * PART : (at + 1) * PART, :]
    group = lax.rem(lax.axis_index("tp") + 4, 8)
    group = pl.ds(pl.multiple_of(group * CHUNK, CHUNK), CHUNK)
    product[...] = jnp.dot(
        attention[...], weight[:, group], preferred_element_type=F32
    ).astype(BF16)


def project_kernel(own, mate, weight, *outs):
    both = jnp.concatenate([own[...], mate[...]], axis=0)
    side = 1 - 2 * place()[1]
    for at, out in enumerate(outs):
        if out.shape[0] == 2 * PART:
            rows, group = both, lax.axis_index("tp") + 4 + (at + 1) * side
        else:
            rows, group = own[...], lax.axis_index("tp")
        group = lax.rem(group, 8)
        group = pl.ds(pl.multiple_of(group * CHUNK, CHUNK), CHUNK)
        out[...] = jnp.dot(rows, weight[:, group], preferred_element_type=F32).astype(BF16)


def finish_kernel(*refs):
    out = refs[-1]
    for part in range(TOK // PART):
        mine, moved, other = refs[3 * part : 3 * part + 3]
        total = mine[...].astype(F32) + moved[...].astype(F32) + other[...].astype(F32)
        out[pl.ds(part * PART, PART), :] = total.astype(BF16)


VMEM = pl.BlockSpec(memory_space=pltpu.VMEM)
PARAMS = pltpu.CompilerParams(vmem_limit_bytes=12 << 20)


def shape(rows, columns, kind=BF16):
    return jax.ShapeDtypeStruct((rows, columns), kind)


def call(kernel, name, micros, outs, *args, scratch=()):
    return pl.pallas_call(
        kernel,
        out_shape=outs,
        in_specs=[VMEM] * len(args),
        out_specs=[VMEM] * len(outs) if isinstance(outs, list) else VMEM,
        scratch_shapes=list(scratch),
        compiler_params=PARAMS,
        cost_estimate=pl.CostEstimate(
            flops=int(micros * 1e9), bytes_accessed=1 << 10, transcendentals=0
        ),
        name=name,
    )(*args)


def kept_shapes(count):
    return [shape(ROWS, count * TOK, F32), shape(ROWS, HD, F32), shape(count * TOK, 2 * HD)]


def per_device(queries, key_values, prompt_ids, out_weight):
    stretches, ring = lax.axis_size("loop"), lax.axis_size("tp")

    def to_mate(value):
        return lax.ppermute(value, "loop", [(i, i ^ 1) for i in range(stretches)])

    def from_chip(value, steps):
        pairs = [(i, (i + 2 * steps) % stretches) for i in range(stretches)]
        return lax.ppermute(value, "loop", pairs)

    def along_row(value, steps):
        pairs = [(i, i // 8 * 8 + (i + 2 * steps) % 8) for i in range(stretches)]
        return lax.ppermute(value, "loop", pairs)

    def along(value, swap=0):
        pairs = []
        for loop in range(stretches):
            step = 1 if loop % 2 else ring - 1
            for z in range(ring):
                pairs.append((loop * ring + z, (loop ^ swap) * ring + (z + step) % ring))
        return lax.ppermute(value, ("loop", "tp"), pairs)

    piece = shape(PIECE, TOK)
    column = shape(TOK, 1, F32)
    own = call(pack_kernel, "pack", 0.05, piece, key_values, prompt_ids.astype(F32)[None, :])
    chip4 = from_chip(own, 4)
    again, ids = call(column_kernel, "column", 0.05, [piece, column], own)
    query_rows, *kept = call(
        own_kernel, "own_scores", 0.1, [shape(ROWS, HD)] + kept_shapes(1), queries, ids, again
    )
    (chip4, kept) = lax.optimization_barrier((chip4, kept))
    beside, ids, *relayed = call(
        pick_kernel, "pick", 0.05, [piece, column, piece, piece, piece], again, chip4, ids
    )
    chip1, chip2, chip3 = [along_row(relayed[s - 1], s) for s in (1, 2, 3)]
    beside = to_mate(beside)
    pieces = [(4, chip4)]
    state = call(
        functools.partial(fold_kernel, [item[0] for item in pieces], 1),
        "fold",
        3.0,
        [shape(ROWS, HD, F32), shape(ROWS, 2 * HD, F32)],
        query_rows,
        ids,
        *[item[1] for item in pieces],
        *kept,
        scratch=later(1),
    )
    (chip1, chip2, chip3, state) = lax.optimization_barrier((chip1, chip2, chip3, state))
    mate1, mate2, mate3 = [to_mate(chip) for chip in (chip1, chip2, chip3)]
    pieces = [(BESIDE, beside), (1, chip1), (2, chip2), (3, chip3)]
    kept = call(
        functools.partial(more_kernel, [item[0] for item in pieces]),
        "more_scores",
        3.0,
        kept_shapes(4),
        query_rows,
        ids,
        *[item[1] for item in pieces],
    )

    ends = []
    for part in range(TOK // PART):
        attention, product = call(
            functools.partial(last_kernel, part, [1, 2, 3], 1),
            "attend",
            0.01,
            [shape(PART, HEADS * HD), shape(PART, CHUNK)],
            query_rows,
            ids,
            mate1,
            mate2,
            mate3,
            *kept,
            *state,
            out_weight,
            scratch=later(3),
        )
        extra = along(product)
        wide = shape(2 * PART, CHUNK)
        one, two, three, mine = call(
            project_kernel,
            "project",
            0.01,
            [wide, wide, wide, shape(PART, CHUNK)],
            attention,
            to_mate(attention),
            out_weight,
        )
        moved = along(jnp.concatenate([one[:PART] + extra, one[PART:]], axis=0))
        moved = along(two + moved)
        ends += [mine, along(three[:PART] + moved[:PART])]
        ends += [along(three[PART:] + moved[PART:], swap=1)]
    return call(finish_kernel, "finish", 0.5, shape(TOK, CHUNK), *ends)


def later(count):
    return [
        pltpu.VMEM((HEADS * PART, count * TOK), F32),
        pltpu.VMEM((HEADS * PART, HD), F32),
        pltpu.VMEM((count * TOK, 2 * HD), BF16),
    ]


def solution(mesh):
    in_specs = (P("loop", "tp"), P("loop", "tp"), P("loop"), P("tp", None))
    out_specs = P("loop", "tp")
    return jax.shard_map(
        per_device, mesh=mesh, in_specs=in_specs, out_specs=out_specs, check_vma=False
    )
```

```python
import functools
import math

import jax
import jax.numpy as jnp
from jax import lax
from jax.experimental import pallas as pl
from jax.experimental.pallas import tpu as pltpu
from jax.sharding import PartitionSpec as P

HD = 128
HEADS = 8
TOK = 256
PART = 128
ROWS = HEADS * TOK
STEP = 256
PIECE = TOK + 16
CHUNK = 512
SCALE = 1.0 / math.sqrt(HD)
MASKED = -1e30
F32 = jnp.float32
BF16 = jnp.bfloat16
BESIDE = -1


def place():
    at = lax.axis_index("loop")
    return at // 2, at % 2


def usable(back):
    chip, core = place()
    if back == 0:
        return jnp.bool_(True)
    if back == BESIDE:
        return (chip >= 4) | (core == 1)
    return chip >= back


def write_piece(out, rows, ids):
    out[0:TOK, :] = rows
    out[TOK:PIECE, :] = jnp.broadcast_to(ids, (PIECE - TOK, TOK)).astype(BF16)


def pack_kernel(key_values, ids, message, column):
    write_piece(message, key_values[...], ids[...])
    square = (TOK, TOK)
    diagonal = lax.broadcasted_iota(jnp.int32, square, 0) == lax.broadcasted_iota(
        jnp.int32, square, 1
    )
    wide = jnp.broadcast_to(ids[...], square)
    column[...] = jnp.sum(jnp.where(diagonal, wide, 0.0), axis=1, keepdims=True)


def pick_kernel(own, far, far_ids, ids, beside, ids_again, packed, *relayed):
    chip, core = place()
    ids_again[...] = ids[...]
    write_piece(packed, far[...], far_ids[...])

    for at, piece in enumerate(relayed):
        inside = chip % 4 + at + 1 < 4

        @pl.when(inside)
        def _(piece=piece):
            piece[...] = own[...]

        @pl.when(jnp.logical_not(inside))
        def _(piece=piece):
            piece[...] = packed[...]

    @pl.when(core == 0)
    def _():
        beside[...] = own[...]

    @pl.when(core != 0)
    def _():
        beside[...] = packed[...]


def find_scores(query_rows, ids, part, pieces, scores, peak, base):
    own_ids = ids[pl.ds(part * PART, PART), :]
    own_ids = jnp.concatenate([own_ids] * (STEP // PART), axis=0)
    names = []
    for back, piece in pieces:
        key_ids = piece[TOK:PIECE, :][0:1, :].astype(F32)
        names.append(jnp.where(usable(back), key_ids, -1.0))
    for step in range(HEADS * PART // STEP):
        rows = pl.ds(part * HEADS * PART + step * STEP, STEP)
        out = pl.ds(base + step * STEP, STEP)
        best = None
        for at, (back, piece) in enumerate(pieces):
            found = lax.dot_general(
                query_rows[rows, :],
                piece[0:TOK, 0:HD],
                (((1,), (1,)), ((), ())),
                preferred_element_type=F32,
            )
            allowed = own_ids == names[at]
            if back == 0:
                shape = (STEP, TOK)
                token = lax.broadcasted_iota(jnp.int32, shape, 0) % PART + part * PART
                allowed = allowed & (lax.broadcasted_iota(jnp.int32, shape, 1) <= token)
            found = jnp.where(allowed, found, MASKED)
            scores[out, at * TOK : (at + 1) * TOK] = found
            here = jnp.maximum(found[:, :HD], found[:, HD:])
            best = here if best is None else jnp.maximum(best, here)
        peak[out, :] = best


def keep_values(pieces, values):
    for at, (_, piece) in enumerate(pieces):
        values[at * TOK : (at + 1) * TOK, 0:HD] = piece[0:TOK, HD:]
    values[:, HD:] = jnp.ones((values.shape[0], HD), BF16)


def own_kernel(queries, ids, piece, query_rows, scores, peak, values):
    for part in range(TOK // PART):
        for head in range(HEADS):
            rows = pl.ds((part * HEADS + head) * PART, PART)
            query_rows[rows, :] = queries[pl.ds(part * PART, PART), pl.ds(head * HD, HD)]
    keep_values([(0, piece)], values)
    for part in range(TOK // PART):
        find_scores(query_rows, ids, part, [(0, piece)], scores, peak, part * HEADS * PART)


def weigh(part, step, scored, folded):
    given = pl.ds(part * HEADS * PART + step * STEP, STEP)
    within = pl.ds(step * STEP, STEP)
    top, blocks = None, []
    for scores, peak, values in scored:
        rows = given if scores.shape[0] == ROWS else within
        best = peak[rows, :]
        top = best if top is None else jnp.maximum(top, best)
        blocks.append((scores, rows, values))
    top = jnp.broadcast_to(jnp.max(top, axis=1, keepdims=True), (STEP, HD))
    total = None
    if folded is not None:
        old = folded[0][given, :]
        top = jnp.maximum(top, old)
        shrink = jnp.exp((old - top) * SCALE)
        total = folded[1][given, :] * jnp.concatenate([shrink, shrink], axis=1)
    for scores, rows, values in blocks:
        wide = jnp.concatenate([top] * (scores.shape[1] // HD), axis=1)
        probs = jnp.exp((scores[rows, :] - wide) * SCALE).astype(BF16)
        added = jnp.dot(probs, values[...], preferred_element_type=F32)
        total = added if total is None else total + added
    return top, total


def fold_kernel(backs, early, has_state, query_rows, ids, *refs):
    pieces = list(zip(backs, refs[: len(backs)]))
    refs = refs[len(backs) :]
    kept = [refs[3 * at : 3 * at + 3] for at in range(early)]
    refs = refs[3 * early :]
    folded = refs[:2] if has_state else None
    tops, sums, scores, peak, values = refs[2 * has_state :]
    keep_values(pieces, values)
    for part in range(TOK // PART):
        find_scores(query_rows, ids, part, pieces, scores, peak, 0)
        for step in range(HEADS * PART // STEP):
            rows = pl.ds(part * HEADS * PART + step * STEP, STEP)
            top, total = weigh(part, step, kept + [(scores, peak, values)], folded)
            tops[rows, :] = top
            sums[rows, :] = total


def more_kernel(backs, query_rows, ids, *refs):
    pieces = list(zip(backs, refs[: len(backs)]))
    scores, peak, values = refs[len(backs) :]
    keep_values(pieces, values)
    for part in range(TOK // PART):
        find_scores(query_rows, ids, part, pieces, scores, peak, part * HEADS * PART)


def last_kernel(part, backs, early, query_rows, ids, *refs):
    pieces = list(zip(backs, refs[: len(backs)]))
    refs = refs[len(backs) :]
    kept = [refs[3 * at : 3 * at + 3] for at in range(early)]
    tops, sums, weight, attention, product, scores, peak, values = refs[3 * early :]
    keep_values(pieces, values)
    find_scores(query_rows, ids, part, pieces, scores, peak, 0)
    for step in range(HEADS * PART // STEP):
        _, total = weigh(part, step, kept + [(scores, peak, values)], (tops, sums))
        share = (total[:, :HD] / total[:, HD:]).astype(BF16)
        for at in range(STEP // PART):
            head = step * (STEP // PART) + at
            attention[:, pl.ds(head * HD, HD)] = share[at * PART : (at + 1) * PART, :]
    group = lax.rem(lax.axis_index("tp") + 4, 8)
    group = pl.ds(pl.multiple_of(group * CHUNK, CHUNK), CHUNK)
    product[...] = jnp.dot(
        attention[...], weight[:, group], preferred_element_type=F32
    ).astype(BF16)


def project_kernel(own, mate, weight, *outs):
    both = jnp.concatenate([own[...], mate[...]], axis=0)
    side = 1 - 2 * place()[1]
    for at, out in enumerate(outs):
        if out.shape[0] == 2 * PART:
            rows, group = both, lax.axis_index("tp") + 4 + (at + 1) * side
        else:
            rows, group = own[...], lax.axis_index("tp")
        group = lax.rem(group, 8)
        group = pl.ds(pl.multiple_of(group * CHUNK, CHUNK), CHUNK)
        out[...] = jnp.dot(rows, weight[:, group], preferred_element_type=F32).astype(BF16)


def finish_kernel(*refs):
    out = refs[-1]
    for part in range(TOK // PART):
        mine, moved, other = refs[3 * part : 3 * part + 3]
        total = mine[...].astype(F32) + moved[...].astype(F32) + other[...].astype(F32)
        out[pl.ds(part * PART, PART), :] = total.astype(BF16)


VMEM = pl.BlockSpec(memory_space=pltpu.VMEM)
PARAMS = pltpu.CompilerParams(vmem_limit_bytes=12 << 20)


def shape(rows, columns, kind=BF16):
    return jax.ShapeDtypeStruct((rows, columns), kind)


def call(kernel, name, micros, outs, *args, scratch=(), aliases={}):
    return pl.pallas_call(
        kernel,
        out_shape=outs,
        in_specs=[VMEM] * len(args),
        out_specs=[VMEM] * len(outs) if isinstance(outs, list) else VMEM,
        scratch_shapes=list(scratch),
        input_output_aliases=aliases,
        compiler_params=PARAMS,
        cost_estimate=pl.CostEstimate(
            flops=int(micros * 1e9), bytes_accessed=1 << 10, transcendentals=0
        ),
        name=name,
    )(*args)


def kept_shapes(count):
    return [shape(ROWS, count * TOK, F32), shape(ROWS, HD, F32), shape(count * TOK, 2 * HD)]


def per_device(queries, key_values, prompt_ids, out_weight):
    stretches, ring = lax.axis_size("loop"), lax.axis_size("tp")

    def to_mate(value):
        return lax.ppermute(value, "loop", [(i, i ^ 1) for i in range(stretches)])

    def from_chip(value, steps):
        pairs = [(i, (i + 2 * steps) % stretches) for i in range(stretches)]
        return lax.ppermute(value, "loop", pairs)

    def along_row(value, steps):
        pairs = [(i, i // 8 * 8 + (i + 2 * steps) % 8) for i in range(stretches)]
        return lax.ppermute(value, "loop", pairs)

    def along(value, swap=0):
        pairs = []
        for loop in range(stretches):
            step = 1 if loop % 2 else ring - 1
            for z in range(ring):
                pairs.append((loop * ring + z, (loop ^ swap) * ring + (z + step) % ring))
        return lax.ppermute(value, ("loop", "tp"), pairs)

    piece = shape(PIECE, TOK)
    column = shape(TOK, 1, F32)
    far = from_chip(key_values, 4)
    row = prompt_ids.astype(F32)[None, :]
    far_ids = from_chip(row, 4)
    own, ids = call(pack_kernel, "pack", 0.1, [piece, column], key_values, row)
    query_rows, *kept = call(
        own_kernel, "own_scores", 0.1, [shape(ROWS, HD)] + kept_shapes(1), queries, ids, own
    )
    (far, kept) = lax.optimization_barrier((far, kept))
    beside, ids, chip4, *relayed = call(
        pick_kernel, "pick", 0.05, [piece, column] + [piece] * 4, own, far, far_ids, ids
    )
    chip1, chip2, chip3 = [along_row(relayed[s - 1], s) for s in (1, 2, 3)]
    beside = to_mate(beside)

    def fold(pieces, kept, state):
        fixed = 2 + len(pieces) + len(kept)
        return call(
            functools.partial(
                fold_kernel, [item[0] for item in pieces], len(kept) // 3, bool(state)
            ),
            "fold",
            0.01,
            [shape(ROWS, HD, F32), shape(ROWS, 2 * HD, F32)],
            query_rows,
            ids,
            *[item[1] for item in pieces],
            *kept,
            *state,
            scratch=later(len(pieces)),
            aliases={fixed: 0, fixed + 1: 1} if state else {},
        )

    state = fold([(4, chip4)], kept, [])
    (chip1, beside, state) = lax.optimization_barrier((chip1, beside, state))
    state = fold([(BESIDE, beside), (1, chip1)], [], state)
    (chip2, state) = lax.optimization_barrier((chip2, state))
    state = fold([(2, chip2)], [], state)
    (chip3, state) = lax.optimization_barrier((chip3, state))
    mate1, mate2, mate3 = [to_mate(chip) for chip in (chip1, chip2, chip3)]
    pieces = [(3, chip3), (1, mate1), (2, mate2)]
    kept = call(
        functools.partial(more_kernel, [item[0] for item in pieces]),
        "more_scores",
        1.5,
        kept_shapes(len(pieces)),
        query_rows,
        ids,
        *[item[1] for item in pieces],
    )

    ends = []
    for part in range(TOK // PART):
        attention, product = call(
            functools.partial(last_kernel, part, [3], 1),
            "attend",
            0.01,
            [shape(PART, HEADS * HD), shape(PART, CHUNK)],
            query_rows,
            ids,
            mate3,
            *kept,
            *state,
            out_weight,
            scratch=later(1),
        )
        extra = along(product)
        wide = shape(2 * PART, CHUNK)
        one, two, three, mine = call(
            project_kernel,
            "project",
            0.01,
            [wide, wide, wide, shape(PART, CHUNK)],
            attention,
            to_mate(attention),
            out_weight,
        )
        moved = along(jnp.concatenate([one[:PART] + extra, one[PART:]], axis=0))
        moved = along(two + moved)
        ends += [mine, along(three[:PART] + moved[:PART])]
        ends += [along(three[PART:] + moved[PART:], swap=1)]
    return call(finish_kernel, "finish", 0.5, shape(TOK, CHUNK), *ends)


def later(count):
    return [
        pltpu.VMEM((HEADS * PART, count * TOK), F32),
        pltpu.VMEM((HEADS * PART, HD), F32),
        pltpu.VMEM((count * TOK, 2 * HD), BF16),
    ]


def solution(mesh):
    in_specs = (P("loop", "tp"), P("loop", "tp"), P("loop"), P("tp", None))
    out_specs = P("loop", "tp")
    return jax.shard_map(
        per_device, mesh=mesh, in_specs=in_specs, out_specs=out_specs, check_vma=False
    )
```

```python
import functools
import math

import jax
import jax.numpy as jnp
from jax import lax
from jax.experimental import pallas as pl
from jax.experimental.pallas import tpu as pltpu
from jax.sharding import PartitionSpec as P

HD = 128
HEADS = 8
TOK = 256
PART = 128
ROWS = HEADS * TOK
STEP = 256
PIECE = TOK + 16
CHUNK = 512
SCALE = math.log2(math.e) / math.sqrt(HD)
MASKED = -1e30
F32 = jnp.float32
BF16 = jnp.bfloat16
BESIDE = -1


def place():
    at = lax.axis_index("loop")
    return at // 2, at % 2


def usable(back):
    chip, core = place()
    if back == 0:
        return jnp.bool_(True)
    if back == BESIDE:
        return (chip >= 4) | (core == 1)
    return chip >= back


def write_piece(out, rows, ids):
    out[0:TOK, :] = rows
    out[TOK:PIECE, :] = jnp.broadcast_to(ids, (PIECE - TOK, TOK)).astype(BF16)


def pack_kernel(key_values, ids, message, column):
    write_piece(message, key_values[...], ids[...])
    square = (TOK, TOK)
    diagonal = lax.broadcasted_iota(jnp.int32, square, 0) == lax.broadcasted_iota(
        jnp.int32, square, 1
    )
    wide = jnp.broadcast_to(ids[...], square)
    column[...] = jnp.sum(jnp.where(diagonal, wide, 0.0), axis=1, keepdims=True)


def pick_kernel(own, far, far_ids, ids, beside, ids_again, packed, *relayed):
    chip, core = place()
    ids_again[...] = ids[...]
    write_piece(packed, far[...], far_ids[...])

    for steps, piece in zip((1, 3), relayed):
        inside = chip % 4 + steps < 4

        @pl.when(inside)
        def _(piece=piece):
            piece[...] = own[...]

        @pl.when(jnp.logical_not(inside))
        def _(piece=piece):
            piece[...] = packed[...]

    @pl.when(core == 0)
    def _():
        beside[...] = own[...]

    @pl.when(core != 0)
    def _():
        beside[...] = packed[...]


def find_scores(query_rows, ids, part, pieces, scores, peak, base):
    own_ids = ids[pl.ds(part * PART, PART), :]
    own_ids = jnp.concatenate([own_ids] * (STEP // PART), axis=0)
    names = []
    for back, piece in pieces:
        key_ids = piece[TOK:PIECE, :][0:1, :].astype(F32)
        names.append(jnp.where(usable(back), key_ids, -1.0))
    for step in range(HEADS * PART // STEP):
        rows = pl.ds(part * HEADS * PART + step * STEP, STEP)
        out = pl.ds(base + step * STEP, STEP)
        best = None
        for at, (back, piece) in enumerate(pieces):
            found = lax.dot_general(
                query_rows[rows, :],
                piece[0:TOK, 0:HD],
                (((1,), (1,)), ((), ())),
                preferred_element_type=F32,
            )
            allowed = own_ids == names[at]
            if back == 0:
                shape = (STEP, TOK)
                token = lax.broadcasted_iota(jnp.int32, shape, 0) % PART + part * PART
                allowed = allowed & (lax.broadcasted_iota(jnp.int32, shape, 1) <= token)
            found = jnp.where(allowed, found, MASKED)
            scores[out, at * TOK : (at + 1) * TOK] = found
            here = jnp.maximum(found[:, :HD], found[:, HD:])
            best = here if best is None else jnp.maximum(best, here)
        peak[out, :] = best


def keep_values(pieces, values):
    for at, (_, piece) in enumerate(pieces):
        values[at * TOK : (at + 1) * TOK, 0:HD] = piece[0:TOK, HD:]
    values[:, HD:] = jnp.ones((values.shape[0], HD), BF16)


def own_kernel(queries, ids, piece, query_rows, scores, peak, values):
    for part in range(TOK // PART):
        for head in range(HEADS):
            rows = pl.ds((part * HEADS + head) * PART, PART)
            query_rows[rows, :] = queries[pl.ds(part * PART, PART), pl.ds(head * HD, HD)]
    keep_values([(0, piece)], values)
    for part in range(TOK // PART):
        find_scores(query_rows, ids, part, [(0, piece)], scores, peak, part * HEADS * PART)


def weigh(part, step, scored, folded):
    given = pl.ds(part * HEADS * PART + step * STEP, STEP)
    within = pl.ds(step * STEP, STEP)
    top, blocks = None, []
    for scores, peak, values in scored:
        rows = given if scores.shape[0] == ROWS else within
        best = peak[rows, :]
        top = best if top is None else jnp.maximum(top, best)
        blocks.append((scores, rows, values))
    top = jnp.broadcast_to(jnp.max(top, axis=1, keepdims=True), (STEP, HD))
    total = None
    if folded is not None:
        old = folded[0][given, :]
        top = jnp.maximum(top, old)
        shrink = jnp.exp2((old - top) * SCALE)
        total = folded[1][given, :] * jnp.concatenate([shrink, shrink], axis=1)
    for scores, rows, values in blocks:
        wide = jnp.concatenate([top] * (scores.shape[1] // HD), axis=1)
        probs = jnp.exp2((scores[rows, :] - wide) * SCALE).astype(BF16)
        added = jnp.dot(probs, values[...], preferred_element_type=F32)
        total = added if total is None else total + added
    return top, total


def fold_kernel(backs, early, has_state, query_rows, ids, *refs):
    pieces = list(zip(backs, refs[: len(backs)]))
    refs = refs[len(backs) :]
    kept = [refs[3 * at : 3 * at + 3] for at in range(early)]
    refs = refs[3 * early :]
    folded = refs[:2] if has_state else None
    tops, sums, scores, peak, values = refs[2 * has_state :]
    keep_values(pieces, values)
    for part in range(TOK // PART):
        find_scores(query_rows, ids, part, pieces, scores, peak, 0)
        for step in range(HEADS * PART // STEP):
            rows = pl.ds(part * HEADS * PART + step * STEP, STEP)
            top, total = weigh(part, step, kept + [(scores, peak, values)], folded)
            tops[rows, :] = top
            sums[rows, :] = total


def more_kernel(backs, query_rows, ids, *refs):
    pieces = list(zip(backs, refs[: len(backs)]))
    scores, peak, values = refs[len(backs) :]
    keep_values(pieces, values)
    for part in range(TOK // PART):
        find_scores(query_rows, ids, part, pieces, scores, peak, part * HEADS * PART)


def last_kernel(part, backs, early, query_rows, ids, *refs):
    pieces = list(zip(backs, refs[: len(backs)]))
    refs = refs[len(backs) :]
    kept = [refs[3 * at : 3 * at + 3] for at in range(early)]
    tops, sums, weight, attention, product, scores, peak, values = refs[3 * early :]
    keep_values(pieces, values)
    find_scores(query_rows, ids, part, pieces, scores, peak, 0)
    for step in range(HEADS * PART // STEP):
        _, total = weigh(part, step, kept + [(scores, peak, values)], (tops, sums))
        share = (total[:, :HD] / total[:, HD:]).astype(BF16)
        for at in range(STEP // PART):
            head = step * (STEP // PART) + at
            attention[:, pl.ds(head * HD, HD)] = share[at * PART : (at + 1) * PART, :]
    group = lax.rem(lax.axis_index("tp") + 4, 8)
    group = pl.ds(pl.multiple_of(group * CHUNK, CHUNK), CHUNK)
    product[...] = jnp.dot(
        attention[...], weight[:, group], preferred_element_type=F32
    ).astype(BF16)


def project_kernel(own, mate, weight, *outs):
    both = jnp.concatenate([own[...], mate[...]], axis=0)
    side = 1 - 2 * place()[1]
    for at, out in enumerate(outs):
        if out.shape[0] == 2 * PART:
            rows, group = both, lax.axis_index("tp") + 4 + (at + 1) * side
        else:
            rows, group = own[...], lax.axis_index("tp")
        group = lax.rem(group, 8)
        group = pl.ds(pl.multiple_of(group * CHUNK, CHUNK), CHUNK)
        out[...] = jnp.dot(rows, weight[:, group], preferred_element_type=F32).astype(BF16)


def finish_kernel(*refs):
    out = refs[-1]
    for part in range(TOK // PART):
        mine, moved, other = refs[3 * part : 3 * part + 3]
        total = mine[...].astype(F32) + moved[...].astype(F32) + other[...].astype(F32)
        out[pl.ds(part * PART, PART), :] = total.astype(BF16)


VMEM = pl.BlockSpec(memory_space=pltpu.VMEM)
PARAMS = pltpu.CompilerParams(vmem_limit_bytes=12 << 20)


def shape(rows, columns, kind=BF16):
    return jax.ShapeDtypeStruct((rows, columns), kind)


def call(kernel, name, micros, outs, *args, scratch=(), aliases={}):
    return pl.pallas_call(
        kernel,
        out_shape=outs,
        in_specs=[VMEM] * len(args),
        out_specs=[VMEM] * len(outs) if isinstance(outs, list) else VMEM,
        scratch_shapes=list(scratch),
        input_output_aliases=aliases,
        compiler_params=PARAMS,
        cost_estimate=pl.CostEstimate(
            flops=int(micros * 1e9), bytes_accessed=1 << 10, transcendentals=0
        ),
        name=name,
    )(*args)


def kept_shapes(count):
    return [shape(ROWS, count * TOK, F32), shape(ROWS, HD, F32), shape(count * TOK, 2 * HD)]


def per_device(queries, key_values, prompt_ids, out_weight):
    stretches, ring = lax.axis_size("loop"), lax.axis_size("tp")

    def to_mate(value):
        return lax.ppermute(value, "loop", [(i, i ^ 1) for i in range(stretches)])

    def from_chip(value, steps):
        pairs = [(i, (i + 2 * steps) % stretches) for i in range(stretches)]
        return lax.ppermute(value, "loop", pairs)

    def along_row(value, steps):
        pairs = [(i, i // 8 * 8 + (i + 2 * steps) % 8) for i in range(stretches)]
        return lax.ppermute(value, "loop", pairs)

    def along(value, swap=0):
        pairs = []
        for loop in range(stretches):
            step = 1 if loop % 2 else ring - 1
            for z in range(ring):
                pairs.append((loop * ring + z, (loop ^ swap) * ring + (z + step) % ring))
        return lax.ppermute(value, ("loop", "tp"), pairs)

    piece = shape(PIECE, TOK)
    column = shape(TOK, 1, F32)
    far = from_chip(key_values, 4)
    row = prompt_ids.astype(F32)[None, :]
    far_ids = from_chip(row, 4)
    own, ids = call(pack_kernel, "pack", 0.1, [piece, column], key_values, row)
    chip2 = from_chip(own, 2)
    query_rows, *kept = call(
        own_kernel, "own_scores", 0.1, [shape(ROWS, HD)] + kept_shapes(1), queries, ids, own
    )
    (far, kept) = lax.optimization_barrier((far, kept))
    beside, ids, chip4, *relayed = call(
        pick_kernel, "pick", 0.05, [piece, column] + [piece] * 3, own, far, far_ids, ids
    )
    chip1, chip3 = along_row(relayed[0], 1), along_row(relayed[1], 3)
    beside = to_mate(beside)

    def fold(pieces, kept, state):
        fixed = 2 + len(pieces) + len(kept)
        return call(
            functools.partial(
                fold_kernel, [item[0] for item in pieces], len(kept) // 3, bool(state)
            ),
            "fold",
            2.0,
            [shape(ROWS, HD, F32), shape(ROWS, 2 * HD, F32)],
            query_rows,
            ids,
            *[item[1] for item in pieces],
            *kept,
            *state,
            scratch=later(len(pieces)),
            aliases={fixed: 0, fixed + 1: 1} if state else {},
        )

    state = fold([(4, chip4)], kept, [])
    (chip2, state) = lax.optimization_barrier((chip2, state))
    mate2 = to_mate(chip2)
    state = fold([(BESIDE, beside), (2, chip2)], [], state)
    (chip1, chip3, state) = lax.optimization_barrier((chip1, chip3, state))
    mate1, mate3 = to_mate(chip1), to_mate(chip3)
    pieces = [(2, mate2), (1, chip1), (3, chip3)]
    kept = call(
        functools.partial(more_kernel, [item[0] for item in pieces]),
        "more_scores",
        1.5,
        kept_shapes(len(pieces)),
        query_rows,
        ids,
        *[item[1] for item in pieces],
    )

    ends = []
    for part in range(TOK // PART):
        attention, product = call(
            functools.partial(last_kernel, part, [1, 3], 1),
            "attend",
            0.01,
            [shape(PART, HEADS * HD), shape(PART, CHUNK)],
            query_rows,
            ids,
            mate1,
            mate3,
            *kept,
            *state,
            out_weight,
            scratch=later(2),
        )
        extra = along(product)
        wide = shape(2 * PART, CHUNK)
        one, two, three, mine = call(
            project_kernel,
            "project",
            0.01,
            [wide, wide, wide, shape(PART, CHUNK)],
            attention,
            to_mate(attention),
            out_weight,
        )
        moved = along(jnp.concatenate([one[:PART] + extra, one[PART:]], axis=0))
        moved = along(two + moved)
        ends += [mine, along(three[:PART] + moved[:PART])]
        ends += [along(three[PART:] + moved[PART:], swap=1)]
    return call(finish_kernel, "finish", 0.5, shape(TOK, CHUNK), *ends)


def later(count):
    return [
        pltpu.VMEM((HEADS * PART, count * TOK), F32),
        pltpu.VMEM((HEADS * PART, HD), F32),
        pltpu.VMEM((count * TOK, 2 * HD), BF16),
    ]


def solution(mesh):
    in_specs = (P("loop", "tp"), P("loop", "tp"), P("loop"), P("tp", None))
    out_specs = P("loop", "tp")
    return jax.shard_map(
        per_device, mesh=mesh, in_specs=in_specs, out_specs=out_specs, check_vma=False
    )
```

```python
import functools
import math

import jax
import jax.numpy as jnp
from jax import lax
from jax.experimental import pallas as pl
from jax.experimental.pallas import tpu as pltpu
from jax.sharding import PartitionSpec as P

HD = 128
HEADS = 8
TOK = 256
PART = 128
ROWS = HEADS * TOK
STEP = 256
PIECE = TOK + 16
CHUNK = 512
SCALE = math.log2(math.e) / math.sqrt(HD)
MASKED = -1e30
F32 = jnp.float32
BF16 = jnp.bfloat16
BESIDE = -1


def place():
    at = lax.axis_index("loop")
    return at // 2, at % 2


def usable(back):
    chip, core = place()
    if back == 0:
        return jnp.bool_(True)
    if back == BESIDE:
        return (chip >= 4) | (core == 1)
    return chip >= back


def write_piece(out, rows, ids):
    out[0:TOK, :] = rows
    out[TOK:PIECE, :] = jnp.broadcast_to(ids, (PIECE - TOK, TOK)).astype(BF16)


def pack_kernel(key_values, ids, message, column):
    write_piece(message, key_values[...], ids[...])
    square = (TOK, TOK)
    diagonal = lax.broadcasted_iota(jnp.int32, square, 0) == lax.broadcasted_iota(
        jnp.int32, square, 1
    )
    wide = jnp.broadcast_to(ids[...], square)
    column[...] = jnp.sum(jnp.where(diagonal, wide, 0.0), axis=1, keepdims=True)


def pick_kernel(own, far, far_ids, ids, beside, ids_again, packed, *relayed):
    chip, core = place()
    ids_again[...] = ids[...]
    write_piece(packed, far[...], far_ids[...].astype(F32))

    for steps, piece in zip((1, 3), relayed):
        inside = chip % 4 + steps < 4

        @pl.when(inside)
        def _(piece=piece):
            piece[...] = own[...]

        @pl.when(jnp.logical_not(inside))
        def _(piece=piece):
            piece[...] = packed[...]

    @pl.when(core == 0)
    def _():
        beside[...] = own[...]

    @pl.when(core != 0)
    def _():
        beside[...] = packed[...]


def find_scores(query_rows, ids, part, pieces, scores, peak, base):
    own_ids = ids[pl.ds(part * PART, PART), :]
    own_ids = jnp.concatenate([own_ids] * (STEP // PART), axis=0)
    names = []
    for back, piece in pieces:
        key_ids = piece[TOK:PIECE, :][0:1, :].astype(F32)
        names.append(jnp.where(usable(back), key_ids, -1.0))
    for step in range(HEADS * PART // STEP):
        rows = pl.ds(part * HEADS * PART + step * STEP, STEP)
        out = pl.ds(base + step * STEP, STEP)
        best = None
        for at, (back, piece) in enumerate(pieces):
            found = lax.dot_general(
                query_rows[rows, :],
                piece[0:TOK, 0:HD],
                (((1,), (1,)), ((), ())),
                preferred_element_type=F32,
            )
            allowed = own_ids == names[at]
            if back == 0:
                shape = (STEP, TOK)
                token = lax.broadcasted_iota(jnp.int32, shape, 0) % PART + part * PART
                allowed = allowed & (lax.broadcasted_iota(jnp.int32, shape, 1) <= token)
            found = jnp.where(allowed, found, MASKED)
            scores[out, at * TOK : (at + 1) * TOK] = found
            here = jnp.maximum(found[:, :HD], found[:, HD:])
            best = here if best is None else jnp.maximum(best, here)
        peak[out, :] = best


def keep_values(pieces, values):
    for at, (_, piece) in enumerate(pieces):
        values[at * TOK : (at + 1) * TOK, 0:HD] = piece[0:TOK, HD:]
    values[:, HD:] = jnp.ones((values.shape[0], HD), BF16)


def own_kernel(queries, ids, piece, query_rows, scores, peak, values):
    for part in range(TOK // PART):
        for head in range(HEADS):
            rows = pl.ds((part * HEADS + head) * PART, PART)
            query_rows[rows, :] = queries[pl.ds(part * PART, PART), pl.ds(head * HD, HD)]
    keep_values([(0, piece)], values)
    for part in range(TOK // PART):
        find_scores(query_rows, ids, part, [(0, piece)], scores, peak, part * HEADS * PART)


def weigh(part, step, scored, folded):
    given = pl.ds(part * HEADS * PART + step * STEP, STEP)
    within = pl.ds(step * STEP, STEP)
    top, blocks = None, []
    for scores, peak, values in scored:
        rows = given if scores.shape[0] == ROWS else within
        best = peak[rows, :]
        top = best if top is None else jnp.maximum(top, best)
        blocks.append((scores, rows, values))
    top = jnp.broadcast_to(jnp.max(top, axis=1, keepdims=True), (STEP, HD))
    total = None
    if folded is not None:
        old = folded[0][given, :]
        top = jnp.maximum(top, old)
        shrink = jnp.exp2((old - top) * SCALE)
        total = folded[1][given, :] * jnp.concatenate([shrink, shrink], axis=1)
    for scores, rows, values in blocks:
        wide = jnp.concatenate([top] * (scores.shape[1] // HD), axis=1)
        probs = jnp.exp2((scores[rows, :] - wide) * SCALE).astype(BF16)
        added = jnp.dot(probs, values[...], preferred_element_type=F32)
        total = added if total is None else total + added
    return top, total


def fold_kernel(backs, early, has_state, query_rows, ids, *refs):
    pieces = list(zip(backs, refs[: len(backs)]))
    refs = refs[len(backs) :]
    kept = [refs[3 * at : 3 * at + 3] for at in range(early)]
    refs = refs[3 * early :]
    folded = refs[:2] if has_state else None
    tops, sums, scores, peak, values = refs[2 * has_state :]
    keep_values(pieces, values)
    for part in range(TOK // PART):
        find_scores(query_rows, ids, part, pieces, scores, peak, 0)
        for step in range(HEADS * PART // STEP):
            rows = pl.ds(part * HEADS * PART + step * STEP, STEP)
            top, total = weigh(part, step, kept + [(scores, peak, values)], folded)
            tops[rows, :] = top
            sums[rows, :] = total


def more_kernel(backs, query_rows, ids, *refs):
    pieces = list(zip(backs, refs[: len(backs)]))
    scores, peak, values = refs[len(backs) :]
    keep_values(pieces, values)
    for part in range(TOK // PART):
        find_scores(query_rows, ids, part, pieces, scores, peak, part * HEADS * PART)


def last_kernel(part, backs, early, query_rows, ids, *refs):
    pieces = list(zip(backs, refs[: len(backs)]))
    refs = refs[len(backs) :]
    kept = [refs[3 * at : 3 * at + 3] for at in range(early)]
    tops, sums, weight, attention, product, scores, peak, values = refs[3 * early :]
    keep_values(pieces, values)
    find_scores(query_rows, ids, part, pieces, scores, peak, 0)
    for step in range(HEADS * PART // STEP):
        _, total = weigh(part, step, kept + [(scores, peak, values)], (tops, sums))
        share = (total[:, :HD] / total[:, HD:]).astype(BF16)
        for at in range(STEP // PART):
            head = step * (STEP // PART) + at
            attention[:, pl.ds(head * HD, HD)] = share[at * PART : (at + 1) * PART, :]
    group = lax.rem(lax.axis_index("tp") + 4, 8)
    group = pl.ds(pl.multiple_of(group * CHUNK, CHUNK), CHUNK)
    product[...] = jnp.dot(
        attention[...], weight[:, group], preferred_element_type=F32
    ).astype(BF16)


def project_kernel(own, mate, weight, *outs):
    both = jnp.concatenate([own[...], mate[...]], axis=0)
    side = 1 - 2 * place()[1]
    for at, out in enumerate(outs):
        if out.shape[0] == 2 * PART:
            rows, group = both, lax.axis_index("tp") + 4 + (at + 1) * side
        else:
            rows, group = own[...], lax.axis_index("tp")
        group = lax.rem(group, 8)
        group = pl.ds(pl.multiple_of(group * CHUNK, CHUNK), CHUNK)
        out[...] = jnp.dot(rows, weight[:, group], preferred_element_type=F32).astype(BF16)


def finish_kernel(*refs):
    out = refs[-1]
    for part in range(TOK // PART):
        mine, moved, other = refs[3 * part : 3 * part + 3]
        total = mine[...].astype(F32) + moved[...].astype(F32) + other[...].astype(F32)
        out[pl.ds(part * PART, PART), :] = total.astype(BF16)


VMEM = pl.BlockSpec(memory_space=pltpu.VMEM)
PARAMS = pltpu.CompilerParams(vmem_limit_bytes=12 << 20)


def shape(rows, columns, kind=BF16):
    return jax.ShapeDtypeStruct((rows, columns), kind)


def call(kernel, name, micros, outs, *args, scratch=(), aliases={}):
    return pl.pallas_call(
        kernel,
        out_shape=outs,
        in_specs=[VMEM] * len(args),
        out_specs=[VMEM] * len(outs) if isinstance(outs, list) else VMEM,
        scratch_shapes=list(scratch),
        input_output_aliases=aliases,
        compiler_params=PARAMS,
        cost_estimate=pl.CostEstimate(
            flops=int(micros * 1e9), bytes_accessed=1 << 10, transcendentals=0
        ),
        name=name,
    )(*args)


def kept_shapes(count):
    return [shape(ROWS, count * TOK, F32), shape(ROWS, HD, F32), shape(count * TOK, 2 * HD)]


def per_device(queries, key_values, prompt_ids, out_weight):
    stretches, ring = lax.axis_size("loop"), lax.axis_size("tp")

    def to_mate(value):
        return lax.ppermute(value, "loop", [(i, i ^ 1) for i in range(stretches)])

    def from_chip(value, steps):
        pairs = [(i, (i + 2 * steps) % stretches) for i in range(stretches)]
        return lax.ppermute(value, "loop", pairs)

    def along_row(value, steps):
        pairs = [(i, i // 8 * 8 + (i + 2 * steps) % 8) for i in range(stretches)]
        return lax.ppermute(value, "loop", pairs)

    def along(value, swap=0):
        pairs = []
        for loop in range(stretches):
            step = 1 if loop % 2 else ring - 1
            for z in range(ring):
                pairs.append((loop * ring + z, (loop ^ swap) * ring + (z + step) % ring))
        return lax.ppermute(value, ("loop", "tp"), pairs)

    piece = shape(PIECE, TOK)
    column = shape(TOK, 1, F32)
    far = from_chip(key_values, 4)
    row = prompt_ids.astype(F32)[None, :]
    far_ids = from_chip(prompt_ids[None, :], 4)
    own, ids = call(pack_kernel, "pack", 2.0, [piece, column], key_values, row)
    chip2 = from_chip(own, 2)
    query_rows, *kept = call(
        own_kernel, "own_scores", 0.1, [shape(ROWS, HD)] + kept_shapes(1), queries, ids, own
    )
    (far, kept) = lax.optimization_barrier((far, kept))
    beside, ids, chip4, *relayed = call(
        pick_kernel, "pick", 0.05, [piece, column] + [piece] * 3, own, far, far_ids, ids
    )
    chip1, chip3 = along_row(relayed[0], 1), along_row(relayed[1], 3)
    beside = to_mate(beside)

    def fold(pieces, kept, state):
        fixed = 2 + len(pieces) + len(kept)
        return call(
            functools.partial(
                fold_kernel, [item[0] for item in pieces], len(kept) // 3, bool(state)
            ),
            "fold",
            2.0,
            [shape(ROWS, HD, F32), shape(ROWS, 2 * HD, F32)],
            query_rows,
            ids,
            *[item[1] for item in pieces],
            *kept,
            *state,
            scratch=later(len(pieces)),
            aliases={fixed: 0, fixed + 1: 1} if state else {},
        )

    state = fold([(4, chip4)], kept, [])
    (chip2, state) = lax.optimization_barrier((chip2, state))
    mate2 = to_mate(chip2)
    state = fold([(BESIDE, beside), (2, chip2)], [], state)
    (chip1, chip3, state) = lax.optimization_barrier((chip1, chip3, state))
    mate1, mate3 = to_mate(chip1), to_mate(chip3)
    pieces = [(2, mate2), (1, chip1), (3, chip3)]
    kept = call(
        functools.partial(more_kernel, [item[0] for item in pieces]),
        "more_scores",
        1.5,
        kept_shapes(len(pieces)),
        query_rows,
        ids,
        *[item[1] for item in pieces],
    )

    ends = []
    for part in range(TOK // PART):
        attention, product = call(
            functools.partial(last_kernel, part, [1, 3], 1),
            "attend",
            0.01,
            [shape(PART, HEADS * HD), shape(PART, CHUNK)],
            query_rows,
            ids,
            mate1,
            mate3,
            *kept,
            *state,
            out_weight,
            scratch=later(2),
        )
        extra = along(product)
        wide = shape(2 * PART, CHUNK)
        one, two, three, mine = call(
            project_kernel,
            "project",
            0.01,
            [wide, wide, wide, shape(PART, CHUNK)],
            attention,
            to_mate(attention),
            out_weight,
        )
        moved = along(jnp.concatenate([one[:PART] + extra, one[PART:]], axis=0))
        moved = along(two + moved)
        if part == 0:
            moved = along(three + moved)
            ends += [mine, moved[:PART], to_mate(moved[PART:])]
        else:
            ends += [mine, along(three[:PART] + moved[:PART])]
            ends += [along(three[PART:] + moved[PART:], swap=1)]
    return call(finish_kernel, "finish", 0.5, shape(TOK, CHUNK), *ends)


def later(count):
    return [
        pltpu.VMEM((HEADS * PART, count * TOK), F32),
        pltpu.VMEM((HEADS * PART, HD), F32),
        pltpu.VMEM((count * TOK, 2 * HD), BF16),
    ]


def solution(mesh):
    in_specs = (P("loop", "tp"), P("loop", "tp"), P("loop"), P("tp", None))
    out_specs = P("loop", "tp")
    return jax.shard_map(
        per_device, mesh=mesh, in_specs=in_specs, out_specs=out_specs, check_vma=False
    )
```

```python
import functools
import math

import jax
import jax.numpy as jnp
from jax import lax
from jax.experimental import pallas as pl
from jax.experimental.pallas import tpu as pltpu
from jax.sharding import PartitionSpec as P

HD = 128
HEADS = 8
TOK = 256
PART = 128
ROWS = HEADS * TOK
STEP = 256
PIECE = TOK + 16
CHUNK = 512
SCALE = math.log2(math.e) / math.sqrt(HD)
MASKED = -1e30
F32 = jnp.float32
BF16 = jnp.bfloat16
BESIDE = -1


def place():
    at = lax.axis_index("loop")
    return at // 2, at % 2


def usable(back):
    chip, core = place()
    if back == 0:
        return jnp.bool_(True)
    if back == BESIDE:
        return (chip >= 4) | (core == 1)
    return chip >= back


def write_piece(out, rows, ids):
    out[0:TOK, :] = rows
    out[TOK:PIECE, :] = jnp.broadcast_to(ids, (PIECE - TOK, TOK)).astype(BF16)


def pack_kernel(key_values, ids, message, column):
    write_piece(message, key_values[...], ids[...])
    square = (TOK, TOK)
    diagonal = lax.broadcasted_iota(jnp.int32, square, 0) == lax.broadcasted_iota(
        jnp.int32, square, 1
    )
    wide = jnp.broadcast_to(ids[...], square)
    column[...] = jnp.sum(jnp.where(diagonal, wide, 0.0), axis=1, keepdims=True)


def pick_kernel(own, far, far_ids, ids, beside, ids_again, packed, *relayed):
    chip, core = place()
    ids_again[...] = ids[...]
    write_piece(packed, far[...], far_ids[...].astype(F32))

    for steps, piece in zip((1, 3), relayed):
        inside = chip % 4 + steps < 4

        @pl.when(inside)
        def _(piece=piece):
            piece[...] = own[...]

        @pl.when(jnp.logical_not(inside))
        def _(piece=piece):
            piece[...] = packed[...]

    @pl.when(core == 0)
    def _():
        beside[...] = own[...]

    @pl.when(core != 0)
    def _():
        beside[...] = packed[...]


def find_scores(query_rows, ids, part, pieces, scores, peak, base):
    own_ids = ids[pl.ds(part * PART, PART), :]
    own_ids = jnp.concatenate([own_ids] * (STEP // PART), axis=0)
    names = []
    for back, piece in pieces:
        key_ids = piece[TOK:PIECE, :][0:1, :].astype(F32)
        names.append(jnp.where(usable(back), key_ids, -1.0))
    for step in range(HEADS * PART // STEP):
        rows = pl.ds(part * HEADS * PART + step * STEP, STEP)
        out = pl.ds(base + step * STEP, STEP)
        best = None
        for at, (back, piece) in enumerate(pieces):
            found = lax.dot_general(
                query_rows[rows, :],
                piece[0:TOK, 0:HD],
                (((1,), (1,)), ((), ())),
                preferred_element_type=F32,
            )
            allowed = own_ids == names[at]
            if back == 0:
                shape = (STEP, TOK)
                token = lax.broadcasted_iota(jnp.int32, shape, 0) % PART + part * PART
                allowed = allowed & (lax.broadcasted_iota(jnp.int32, shape, 1) <= token)
            found = jnp.where(allowed, found, MASKED)
            scores[out, at * TOK : (at + 1) * TOK] = found
            here = jnp.maximum(found[:, :HD], found[:, HD:])
            best = here if best is None else jnp.maximum(best, here)
        peak[out, :] = best


def keep_values(pieces, values):
    for at, (_, piece) in enumerate(pieces):
        values[at * TOK : (at + 1) * TOK, 0:HD] = piece[0:TOK, HD:]
    values[:, HD:] = jnp.ones((values.shape[0], HD), BF16)


def own_kernel(queries, ids, piece, query_rows, scores, peak, values):
    for part in range(TOK // PART):
        for head in range(HEADS):
            rows = pl.ds((part * HEADS + head) * PART, PART)
            query_rows[rows, :] = queries[pl.ds(part * PART, PART), pl.ds(head * HD, HD)]
    keep_values([(0, piece)], values)
    for part in range(TOK // PART):
        find_scores(query_rows, ids, part, [(0, piece)], scores, peak, part * HEADS * PART)


def weigh(part, step, scored, folded):
    given = pl.ds(part * HEADS * PART + step * STEP, STEP)
    within = pl.ds(step * STEP, STEP)
    top, blocks = None, []
    for scores, peak, values in scored:
        rows = given if scores.shape[0] == ROWS else within
        best = peak[rows, :]
        top = best if top is None else jnp.maximum(top, best)
        blocks.append((scores, rows, values))
    top = jnp.broadcast_to(jnp.max(top, axis=1, keepdims=True), (STEP, HD))
    total = None
    if folded is not None:
        old = folded[0][given, :]
        top = jnp.maximum(top, old)
        shrink = jnp.exp2((old - top) * SCALE)
        total = folded[1][given, :] * jnp.concatenate([shrink, shrink], axis=1)
    for scores, rows, values in blocks:
        wide = jnp.concatenate([top] * (scores.shape[1] // HD), axis=1)
        probs = jnp.exp2((scores[rows, :] - wide) * SCALE).astype(BF16)
        added = jnp.dot(probs, values[...], preferred_element_type=F32)
        total = added if total is None else total + added
    return top, total


def fold_kernel(backs, early, has_state, query_rows, ids, *refs):
    pieces = list(zip(backs, refs[: len(backs)]))
    refs = refs[len(backs) :]
    kept = [refs[3 * at : 3 * at + 3] for at in range(early)]
    refs = refs[3 * early :]
    folded = refs[:2] if has_state else None
    tops, sums, scores, peak, values = refs[2 * has_state :]
    keep_values(pieces, values)
    for part in range(TOK // PART):
        find_scores(query_rows, ids, part, pieces, scores, peak, 0)
        for step in range(HEADS * PART // STEP):
            rows = pl.ds(part * HEADS * PART + step * STEP, STEP)
            top, total = weigh(part, step, kept + [(scores, peak, values)], folded)
            tops[rows, :] = top
            sums[rows, :] = total


def more_kernel(backs, query_rows, ids, *refs):
    pieces = list(zip(backs, refs[: len(backs)]))
    scores, peak, values = refs[len(backs) :]
    keep_values(pieces, values)
    for part in range(TOK // PART):
        find_scores(query_rows, ids, part, pieces, scores, peak, part * HEADS * PART)


def last_kernel(part, backs, early, query_rows, ids, *refs):
    pieces = list(zip(backs, refs[: len(backs)]))
    refs = refs[len(backs) :]
    kept = [refs[3 * at : 3 * at + 3] for at in range(early)]
    tops, sums, weight, attention, product, scores, peak, values = refs[3 * early :]
    keep_values(pieces, values)
    find_scores(query_rows, ids, part, pieces, scores, peak, 0)
    for step in range(HEADS * PART // STEP):
        _, total = weigh(part, step, kept + [(scores, peak, values)], (tops, sums))
        share = (total[:, :HD] / total[:, HD:]).astype(BF16)
        for at in range(STEP // PART):
            head = step * (STEP // PART) + at
            attention[:, pl.ds(head * HD, HD)] = share[at * PART : (at + 1) * PART, :]
    group = lax.rem(lax.axis_index("tp") + 4, 8)
    group = pl.ds(pl.multiple_of(group * CHUNK, CHUNK), CHUNK)
    product[...] = jnp.dot(
        attention[...], weight[:, group], preferred_element_type=F32
    ).astype(BF16)


def project_kernel(own, mate, weight, *outs):
    both = jnp.concatenate([own[...], mate[...]], axis=0)
    side = 1 - 2 * place()[1]
    for at, out in enumerate(outs):
        if out.shape[0] == 2 * PART:
            rows, group = both, lax.axis_index("tp") + 4 + (at + 1) * side
        else:
            rows, group = own[...], lax.axis_index("tp")
        group = lax.rem(group, 8)
        group = pl.ds(pl.multiple_of(group * CHUNK, CHUNK), CHUNK)
        out[...] = jnp.dot(rows, weight[:, group], preferred_element_type=F32).astype(BF16)


def finish_kernel(*refs):
    out = refs[-1]
    for part in range(TOK // PART):
        mine, moved, other = refs[3 * part : 3 * part + 3]
        total = mine[...].astype(F32) + moved[...].astype(F32) + other[...].astype(F32)
        out[pl.ds(part * PART, PART), :] = total.astype(BF16)


VMEM = pl.BlockSpec(memory_space=pltpu.VMEM)
PARAMS = pltpu.CompilerParams(vmem_limit_bytes=12 << 20)


def shape(rows, columns, kind=BF16):
    return jax.ShapeDtypeStruct((rows, columns), kind)


def call(kernel, name, micros, outs, *args, scratch=(), aliases={}):
    return pl.pallas_call(
        kernel,
        out_shape=outs,
        in_specs=[VMEM] * len(args),
        out_specs=[VMEM] * len(outs) if isinstance(outs, list) else VMEM,
        scratch_shapes=list(scratch),
        input_output_aliases=aliases,
        compiler_params=PARAMS,
        cost_estimate=pl.CostEstimate(
            flops=int(micros * 1e9), bytes_accessed=1 << 10, transcendentals=0
        ),
        name=name,
    )(*args)


def kept_shapes(count):
    return [shape(ROWS, count * TOK, F32), shape(ROWS, HD, F32), shape(count * TOK, 2 * HD)]


def per_device(queries, key_values, prompt_ids, out_weight):
    stretches, ring = lax.axis_size("loop"), lax.axis_size("tp")

    def to_mate(value):
        return lax.ppermute(value, "loop", [(i, i ^ 1) for i in range(stretches)])

    def from_chip(value, steps):
        pairs = [(i, (i + 2 * steps) % stretches) for i in range(stretches)]
        return lax.ppermute(value, "loop", pairs)

    def along_row(value, steps):
        pairs = [(i, i // 8 * 8 + (i + 2 * steps) % 8) for i in range(stretches)]
        return lax.ppermute(value, "loop", pairs)

    def along(value, swap=0):
        pairs = []
        for loop in range(stretches):
            step = 1 if loop % 2 else ring - 1
            for z in range(ring):
                pairs.append((loop * ring + z, (loop ^ swap) * ring + (z + step) % ring))
        return lax.ppermute(value, ("loop", "tp"), pairs)

    piece = shape(PIECE, TOK)
    column = shape(TOK, 1, F32)
    far = from_chip(key_values, 4)
    row = prompt_ids.astype(F32)[None, :]
    far_ids = from_chip(prompt_ids[None, :], 4)
    own, ids = call(pack_kernel, "pack", 1.0, [piece, column], key_values, row)
    chip2 = from_chip(own, 2)
    query_rows, *kept = call(
        own_kernel, "own_scores", 0.1, [shape(ROWS, HD)] + kept_shapes(1), queries, ids, own
    )
    (far, kept) = lax.optimization_barrier((far, kept))
    beside, ids, chip4, *relayed = call(
        pick_kernel, "pick", 0.05, [piece, column] + [piece] * 3, own, far, far_ids, ids
    )
    chip1, chip3 = along_row(relayed[0], 1), along_row(relayed[1], 3)
    beside = to_mate(beside)

    def fold(pieces, kept, state):
        fixed = 2 + len(pieces) + len(kept)
        return call(
            functools.partial(
                fold_kernel, [item[0] for item in pieces], len(kept) // 3, bool(state)
            ),
            "fold",
            2.0,
            [shape(ROWS, HD, F32), shape(ROWS, 2 * HD, F32)],
            query_rows,
            ids,
            *[item[1] for item in pieces],
            *kept,
            *state,
            scratch=later(len(pieces)),
            aliases={fixed: 0, fixed + 1: 1} if state else {},
        )

    state = fold([(4, chip4)], kept, [])
    (chip2, state) = lax.optimization_barrier((chip2, state))
    mate2 = to_mate(chip2)
    state = fold([(BESIDE, beside), (2, chip2)], [], state)
    (chip1, chip3, state) = lax.optimization_barrier((chip1, chip3, state))
    mate1, mate3 = to_mate(chip1), to_mate(chip3)
    pieces = [(2, mate2), (1, chip1), (3, chip3)]
    kept = call(
        functools.partial(more_kernel, [item[0] for item in pieces]),
        "more_scores",
        1.5,
        kept_shapes(len(pieces)),
        query_rows,
        ids,
        *[item[1] for item in pieces],
    )

    ends = []
    for part in range(TOK // PART):
        attention, product = call(
            functools.partial(last_kernel, part, [1, 3], 1),
            "attend",
            0.01,
            [shape(PART, HEADS * HD), shape(PART, CHUNK)],
            query_rows,
            ids,
            mate1,
            mate3,
            *kept,
            *state,
            out_weight,
            scratch=later(2),
        )
        extra = along(product)
        wide = shape(2 * PART, CHUNK)
        one, two, three, mine = call(
            project_kernel,
            "project",
            0.01,
            [wide, wide, wide, shape(PART, CHUNK)],
            attention,
            to_mate(attention),
            out_weight,
        )
        moved = along(jnp.concatenate([one[:PART] + extra, one[PART:]], axis=0))
        moved = along(two + moved)
        if part == 0:
            moved = along(three + moved)
            ends += [mine, moved[:PART], to_mate(moved[PART:])]
        else:
            ends += [mine, along(three[:PART] + moved[:PART])]
            ends += [along(three[PART:] + moved[PART:], swap=1)]
    return call(finish_kernel, "finish", 0.5, shape(TOK, CHUNK), *ends)


def later(count):
    return [
        pltpu.VMEM((HEADS * PART, count * TOK), F32),
        pltpu.VMEM((HEADS * PART, HD), F32),
        pltpu.VMEM((count * TOK, 2 * HD), BF16),
    ]


def solution(mesh):
    in_specs = (P("loop", "tp"), P("loop", "tp"), P("loop"), P("tp", None))
    out_specs = P("loop", "tp")
    return jax.shard_map(
        per_device, mesh=mesh, in_specs=in_specs, out_specs=out_specs, check_vma=False
    )
```
